32 devices in a mesh: obs: 4 (over y, x), cell: 8 (over z, core).
Axes of the slice: x: 2, y: 2, z: 4, core: 2. Of those that a mesh axis runs over, the one named last changes fastest.
Arguments:
- log_k: bfloat16 [1572864, 128], P(('obs', 'cell')), may hold values from -6 to 6
- heads_pred: bfloat16 [16384, 128], P(('obs', 'cell')), may hold values from -6 to 6
- slot_well: int32 [16384], P(('obs', 'cell')), may hold values from 0 to 4095, as said below
- tile_count: int32 [32], P(('obs', 'cell')), may hold values from 16 to 512, as said below
- obs_values: float32 [4096, 128], P(('obs', 'cell')), may hold values from -9 to 9
- obs_std: float32 [4096], P(('obs', 'cell')), may hold values from 0.5 to 2
- loc_blocks: int32 [8, 8], replicated, may hold values from 0 to 31, all different within a row
- taper: float32 [8, 8], replicated, may hold values from 0.3 to 1
- lambdas: float32 [4], replicated, may hold values from 0.1 to 10
Outputs:
- posterior: bfloat16 [1572864, 128], P(('obs', 'cell'))
- change_norms: float32 [32, 4, 128], P(('obs', 'cell'))
The draws below stay inside these ranges and needn't reach their ends.
Inputs may be any that keep to these rules, and one draw needn't show every extreme that they name: `slot_well`: slots below a cell block's count hold the wells lying in that block in increasing order; every well lies in exactly one cell block; other slots hold 0. No cell block holds more than 16 wells of one observation block, and some pairs hold exactly 16. `tile_count`: some cell blocks hold exactly 512 wells. `loc_blocks`: each row names 8 different blocks, and every block is named by some tile.
All inputs are finite; a program needn't handle non-finite values.
Results may differ from the reference program's by a relative error of at most 0.0095.
Values may be sent and summed in bfloat16 or wider, within the bound.
A program may use at most 256 MiB of HBM per device.

```python
import math
import jax
import jax.numpy as jnp
from jax import lax

M = 128
CELL_DEV = 49152
W_DEV = 128
CAP = 16
LOC = 8
NLAM = 4
SLOTS = 512
HOT = 1
WELLS = 4096
CELLS = 1572864
N_CELL = 8
DEVICES = 32


def wells_layout(key):
    device_order = jax.random.permutation(jax.random.fold_in(key, 11), DEVICES)
    owner_keys = jax.random.split(jax.random.fold_in(key, 12), DEVICES)
    inner_order = jax.vmap(lambda k: jax.random.permutation(k, W_DEV))(owner_keys)
    pair_index = (inner_order.reshape(-1) // CAP).astype(jnp.int32)
    owner = jnp.arange(WELLS, dtype=jnp.int32) // W_DEV
    groups = W_DEV // CAP
    cold_total = DEVICES - HOT
    cold_index = (owner * (groups - 1) + pair_index - 1) % cold_total
    hot_source = device_order[owner % HOT]
    cold_source = device_order[HOT + cold_index]
    source = jnp.where(pair_index == 0, hot_source, cold_source).astype(jnp.int32)
    sort_score = source * WELLS + jnp.arange(WELLS, dtype=jnp.int32)
    ordering = jnp.argsort(sort_score).astype(jnp.int32)
    sorted_source = source[ordering]
    counts = jax.ops.segment_sum(jnp.ones((WELLS,), jnp.int32), source, DEVICES)
    starts = jnp.cumsum(counts) - counts
    slot_rank = jnp.arange(WELLS, dtype=jnp.int32) - starts[sorted_source]
    slot_table = jnp.zeros((DEVICES * SLOTS,), jnp.int32).at[sorted_source * SLOTS + slot_rank].set(ordering)
    return (slot_table, counts.astype(jnp.int32))


def draw_slot_well(key, part):
    return wells_layout(key)[0]


def draw_tile_count(key, part):
    return wells_layout(key)[1]


def block_scale(own_key, dims, cuts, least, high):
    level, own = 1.0, jax.random.fold_in(own_key, 6)
    for axis_at, blocks in cuts:
        heights = jnp.exp(jax.random.uniform(jax.random.fold_in(own, axis_at), (blocks,), jnp.float32, least / len(cuts), high / len(cuts)))
        level = level * jnp.repeat(heights, dims[axis_at] // blocks).reshape([-1 if axis == axis_at else 1 for axis in range(len(dims))])
    return level


def picks_of(own_key, rows, amount, top, lift):
    order = jax.random.permutation(jax.random.fold_in(own_key, 1), amount)
    pull = order
    for power in range(3):
        pull = pull * pull // amount
    pull = pull * lift // amount
    tickets = jax.random.randint(jax.random.fold_in(own_key, 2), (rows, amount), 0, 4096) + pull
    fixed_rows = jax.random.permutation(jax.random.fold_in(own_key, 3), rows)[jnp.arange(amount) % rows]
    tickets = jnp.where(jnp.arange(rows)[:, None] == fixed_rows[None, :], 1 << 14, tickets)
    score = tickets * amount + jnp.arange(amount)
    return lax.top_k(score.astype(jnp.int32), top)[1].astype(jnp.int32)


def noise(stream_key, dims, spread, reach, cuts=(), kind=jnp.bfloat16):
    drawn = spread * jax.random.normal(stream_key, dims, jnp.float32)
    if cuts:
        drawn = drawn * block_scale(stream_key, dims, cuts, -0.22, 0.18)
    return jnp.clip(drawn, -reach, reach).astype(kind)


def setup_inputs(seed: int = 0) -> dict:
    seeds = jax.random.split(jax.random.key(seed), 10)
    return {
        "log_k": noise(seeds[0], (CELLS, M), 1.0, 6.0, ((0, 32),)),
        "heads_pred": noise(seeds[1], (DEVICES * SLOTS, M), 1.0, 6.0, ((0, 32),)),
        "slot_well": draw_slot_well(jax.random.fold_in(seeds[9], 71), 0),
        "tile_count": draw_tile_count(jax.random.fold_in(seeds[9], 71), 0),
        "obs_values": noise(seeds[4], (WELLS, M), 1.5, 9.0, ((0, 32),), jnp.float32),
        "obs_std": jnp.clip(jnp.exp(math.log(2.0) - 1.3862944 * jax.random.uniform(seeds[5], (WELLS,), jnp.float32) ** block_scale(seeds[5], (WELLS,), ((0, 32),), -0.2, 0.2)), 0.5, 2.0),
        "loc_blocks": picks_of(seeds[6], N_CELL, DEVICES, LOC, 4096),
        "taper": jnp.clip(jax.random.uniform(seeds[7], (N_CELL, LOC), jnp.float32, 0.3, 1.0), 0.3, 1.0),
        "lambdas": jnp.clip(jnp.exp(jax.random.uniform(seeds[8], (NLAM,), jnp.float32, math.log(0.1), math.log(10.0))), 0.1, 10.0),
    }


def reference(log_k, heads_pred, slot_well, tile_count, obs_values, obs_std, loc_blocks, taper, lambdas):
    is_valid = jnp.arange(SLOTS, dtype=jnp.int32)[None, :] < tile_count[:, None]
    well_index = jnp.where(is_valid, slot_well.reshape(DEVICES, SLOTS), WELLS).reshape(-1).astype(jnp.int32)
    predicted = jnp.zeros((WELLS, M), jnp.float32).at[well_index].set(heads_pred.astype(jnp.float32), mode='drop')
    member_mean = jnp.mean(predicted, axis=1, keepdims=True)
    scaled = (predicted - member_mean) / obs_std[:, None]
    innovation = (obs_values - predicted) / obs_std[:, None]
    joined = jnp.concatenate([scaled, innovation], axis=1).reshape(DEVICES, W_DEV, 2 * M)
    scaled_blocks = scaled.reshape(DEVICES, W_DEV, M)
    block_gram = jnp.einsum('bwi,bwj->bij', scaled_blocks, joined, precision=lax.Precision.HIGHEST)
    matches = (loc_blocks[:, :, None] == jnp.arange(DEVICES, dtype=jnp.int32)[None, None, :]).astype(jnp.float32)
    tile_weights = jnp.sum(taper[:, :, None] * matches, axis=1)
    tile_gram = jnp.einsum('tb,bij->tij', tile_weights, block_gram, precision=lax.Precision.HIGHEST)
    curvature = tile_gram[:, :, :M]
    right_side = tile_gram[:, :, M:]
    identity = jnp.eye(M, dtype=jnp.float32)
    systems = curvature[:, None] + ((1.0 + lambdas) * (M - 1))[None, :, None, None] * identity
    transforms = jnp.linalg.solve(systems, jnp.broadcast_to(right_side[:, None], systems.shape))
    transforms = transforms.astype(jnp.bfloat16)
    joined_transforms = jnp.transpose(transforms, (0, 2, 1, 3)).reshape(N_CELL, M, NLAM * M)
    field_blocks = log_k.reshape(DEVICES, CELL_DEV, M)

    def update_block(inputs):
        block_field, block_index = inputs
        field = block_field.astype(jnp.float32)
        anomalies = (field - jnp.mean(field, axis=1, keepdims=True)).astype(jnp.bfloat16)
        tile_transform = joined_transforms[block_index % N_CELL]
        change = jnp.dot(anomalies.astype(jnp.float32), tile_transform.astype(jnp.float32), preferred_element_type=jnp.float32)
        change = change.reshape(CELL_DEV, NLAM, M)
        updated = (field + change[:, 0, :]).astype(jnp.bfloat16)
        return (updated, jnp.sum(change * change, axis=0))
    posterior, change_norms = lax.map(update_block, (field_blocks, jnp.arange(DEVICES, dtype=jnp.int32)))
    return (posterior.reshape(CELLS, M), change_norms)
```

```python
import functools

import jax
import jax.numpy as jnp
from jax import lax
from jax.experimental import pallas as pl
from jax.experimental.pallas import tpu as pltpu
from jax.sharding import PartitionSpec as P

CAP = 16
PIECES = 4
MESH = pl.DeviceIdType.MESH
HIGHEST = lax.Precision.HIGHEST
F32 = jnp.float32
BF16 = jnp.bfloat16


def dot(a, b, precision=None):
    return jnp.dot(a, b, precision=precision, preferred_element_type=F32)


def dot_rows(a, b, precision=None):
    return lax.dot_general(
        a, b, (((0,), (0,)), ((), ())), precision=precision, preferred_element_type=F32
    )


def divide(x, n):
    if n & (n - 1) == 0:
        return lax.shift_right_logical(x, jnp.full(x.shape, n.bit_length() - 1, x.dtype))
    return x // n


def rows_per_step(total, most):
    step = most
    while total % step:
        step //= 2
    return step


def gram_kernel(
    n_obs, n_cell, loc,
    heads_ref, well_ref, count_ref, obs_ref, std_ref, loc_ref, taper_ref, log_k_ref,
    gram_ref, cov_ref,
    field, send_heads, recv_heads, send_idx, recv_idx, obs_send, obs_all, pred_send, pred_all,
    s_all, d_all, part, bands, band_sum, summed, field_sem, send_sem, recv_sem,
):
    total = n_obs * n_cell
    o, c = lax.axis_index("obs"), lax.axis_index("cell")
    me = o * n_cell + c
    cells, members = field.shape
    wells = obs_ref.shape[0]
    slots = heads_ref.shape[0]
    piece_rows = cells // PIECES

    def piece_copy(p):
        rows = pl.ds(p * piece_rows, piece_rows)
        return pltpu.make_async_copy(log_k_ref.at[rows], field.at[rows], field_sem.at[p])

    for p in range(PIECES):
        piece_copy(p).start()

    barrier = pltpu.get_barrier_semaphore()

    @pl.loop(1, total)
    def _(i):
        to = lax.rem(me + i, total)
        pl.semaphore_signal(
            barrier, inc=1, device_id=(to // n_cell, lax.rem(to, n_cell)), device_id_type=MESH
        )

    well = well_ref[...]
    lane = lax.broadcasted_iota(jnp.int32, (1, slots), 1)
    owner = divide(well, wells)
    place_in = (well - owner * wells + 1).astype(F32)
    owner = jnp.where(lane < count_ref[0], owner, total)
    lane_f = lane.astype(F32)
    group = 8
    rows_now = group * CAP
    row_at = lax.broadcasted_iota(jnp.int32, (rows_now, 1), 0)
    in_group = divide(row_at, CAP)
    rank = (row_at - in_group * CAP).astype(F32)
    well_lane = lax.broadcasted_iota(jnp.int32, (1, wells), 1).astype(F32)

    @pl.loop(0, total // group)
    def _(i):
        dest = in_group + i * group
        start = jnp.sum(jnp.where(owner < dest, 1.0, 0.0), axis=1, keepdims=True)
        hit = jnp.where((owner == dest) & (lane_f == start + rank), 1.0, 0.0)
        rows = pl.ds(pl.multiple_of(i * rows_now, rows_now), rows_now)
        send_heads[rows, :] = dot(hit.astype(BF16), heads_ref[...]).astype(BF16)
        place = jnp.sum(hit * place_in, axis=1, keepdims=True) - 1.0
        ranks = jnp.where(place == well_lane, rank + 1.0, 0.0)
        for q in range(group):
            send_idx[i * group + q] = (
                jnp.sum(ranks[q * CAP : (q + 1) * CAP], axis=0, keepdims=True) - 1.0
            )

    obs_send[:wells, :] = obs_ref[...]
    obs_send[wells:, :] = jnp.broadcast_to(std_ref[...], (8, wells))
    pl.semaphore_wait(barrier, total - 1)

    def head_rows(d):
        return pl.ds(pl.multiple_of(d * CAP, CAP), CAP)

    @pl.loop(1, total)
    def _(i):
        to = lax.rem(me + i, total)
        device = (to // n_cell, lax.rem(to, n_cell))
        pltpu.make_async_remote_copy(
            src_ref=send_heads.at[head_rows(to)], dst_ref=recv_heads.at[head_rows(me)],
            send_sem=send_sem.at[0], recv_sem=recv_sem.at[0],
            device_id=device, device_id_type=MESH,
        ).start()
        pltpu.make_async_remote_copy(
            src_ref=send_idx.at[to], dst_ref=recv_idx.at[me],
            send_sem=send_sem.at[1], recv_sem=recv_sem.at[1],
            device_id=device, device_id_type=MESH,
        ).start()

    pltpu.make_async_copy(
        send_heads.at[head_rows(me)], recv_heads.at[head_rows(me)], recv_sem.at[0]
    ).start()
    pltpu.make_async_copy(send_idx.at[me], recv_idx.at[me], recv_sem.at[1]).start()

    def to_cells(src, dst, at):
        @pl.loop(1, n_cell)
        def _(i):
            pltpu.make_async_remote_copy(
                src_ref=src, dst_ref=dst.at[c], send_sem=send_sem.at[at],
                recv_sem=recv_sem.at[at],
                device_id=(o, lax.rem(c + i, n_cell)), device_id_type=MESH,
            ).start()

        pltpu.make_async_copy(src, dst.at[c], recv_sem.at[at]).start()

    to_cells(obs_send, obs_all, 2)

    ones = jnp.ones((members, members), BF16)
    step_rows = rows_per_step(piece_rows, 1024)
    cov_ref[...] = jnp.zeros_like(cov_ref)

    def covariance(p):
        piece_copy(p).wait()

        @pl.loop(0, piece_rows // step_rows)
        def _(i):
            at = pl.multiple_of(p * piece_rows + i * step_rows, step_rows)
            x = field[pl.ds(at, step_rows), :]
            mean = dot(x, ones) * (1.0 / members)
            anomalies = (x.astype(F32) - mean).astype(BF16)
            cov_ref[...] += dot_rows(anomalies, anomalies)

    def arrived(ref, at):
        pltpu.make_async_copy(ref, ref, recv_sem.at[at]).wait()

    covariance(0)
    arrived(recv_heads, 0)
    arrived(recv_idx, 1)
    ranks_at = lax.broadcasted_iota(jnp.int32, (total, CAP, wells), 1).astype(F32)
    take = jnp.where(recv_idx[...] == ranks_at, 1.0, 0.0).reshape(total * CAP, wells)
    pred_send[...] = dot_rows(take.astype(BF16), recv_heads[...]).astype(BF16)
    to_cells(pred_send, pred_all, 3)

    covariance(1)
    covariance(2)
    arrived(obs_all, 2)
    arrived(pred_all, 3)
    eye = (
        lax.broadcasted_iota(jnp.int32, (wells, wells), 0)
        == lax.broadcasted_iota(jnp.int32, (wells, wells), 1)
    )

    @pl.loop(0, n_cell)
    def _(b):
        block = o * n_cell + b
        weight = jnp.float32(0.0)
        for k in range(loc):
            weight = weight + jnp.where(loc_ref[c, k] == block, taper_ref[c, k], 0.0)
        std = jnp.sum(
            jnp.where(eye, obs_all[b, pl.ds(wells, 1), :], 0.0), axis=1, keepdims=True
        )
        inverse = 1.0 / std
        pred = pred_all[b].astype(F32)
        mean = jnp.mean(pred, axis=1, keepdims=True)
        scaled = (pred - mean) * inverse
        rows = pl.ds(pl.multiple_of(b * wells, wells), wells)
        s_all[rows, :] = scaled * weight
        d_all[rows, :members] = scaled
        d_all[rows, members:] = (obs_all[b, pl.ds(0, wells), :] - pred) * inverse

    product = dot_rows(s_all[...], d_all[...], HIGHEST)
    band = members // n_obs
    part[...] = product.reshape(part.shape)

    def obs_copies(src_of, dst, at):
        @pl.loop(1, n_obs)
        def _(i):
            to = lax.rem(o + i, n_obs)
            pltpu.make_async_remote_copy(
                src_ref=src_of(to), dst_ref=dst.at[o], send_sem=send_sem.at[at],
                recv_sem=recv_sem.at[at], device_id=(to, c), device_id_type=MESH,
            ).start()

        pltpu.make_async_copy(src_of(o), dst.at[o], recv_sem.at[at]).start()

    obs_copies(lambda to: part.at[to], bands, 4)
    arrived(bands, 4)
    band_sum[...] = jnp.sum(bands[...], axis=0)
    obs_copies(lambda to: band_sum, summed, 5)
    covariance(3)
    arrived(summed, 5)
    gram_ref[...] = summed[...].reshape(gram_ref.shape)

    def sent(ref, at):
        pltpu.make_async_copy(ref, ref, send_sem.at[at]).wait()

    sent(recv_heads.at[pl.ds(0, (total - 1) * CAP)], 0)
    sent(recv_idx.at[pl.ds(0, total - 1)], 1)
    sent(obs_all.at[pl.ds(0, n_cell - 1)], 2)
    sent(pred_all.at[pl.ds(0, n_cell - 1)], 3)
    sent(bands.at[pl.ds(0, n_obs - 1)], 4)
    sent(summed.at[pl.ds(0, n_obs - 1)], 5)


def update_kernel(
    gram_ref, cov_ref, lambda_ref, log_k_ref, posterior_ref, norms_ref,
    field, inverse, weights, in_sem, out_sem,
):
    cells, members = field.shape
    groups = in_sem.shape[0]
    group_rows = cells // groups
    lambda_total = lambda_ref.shape[0]

    def group_copy(g, back):
        rows = pl.ds(g * group_rows, group_rows)
        if back:
            return pltpu.make_async_copy(field.at[rows], posterior_ref.at[rows], out_sem.at[g])
        return pltpu.make_async_copy(log_k_ref.at[rows], field.at[rows], in_sem.at[g])

    for g in range(groups):
        group_copy(g, False).start()

    curvature = gram_ref[:, :members]
    top = jnp.max(jnp.sum(jnp.abs(curvature), axis=1, keepdims=True))
    eye = jnp.where(
        lax.broadcasted_iota(jnp.int32, (members, members), 0)
        == lax.broadcasted_iota(jnp.int32, (members, members), 1),
        1.0, 0.0,
    )
    shifts = [(1.0 + lambda_ref[l]) * (members - 1) for l in range(lambda_total)]

    def system(l):
        return gram_ref[:, :members] + shifts[l] * eye

    rhos = []
    for l in range(lambda_total):
        first = 2.0 / (2.0 * shifts[l] + top)
        rho = top * (0.5 * first)
        gain = 2.0 / (2.0 - rho * rho)
        inverse[l] = (gain * first) * (2.0 * eye - first * system(l))
        rhos.append(rho * rho / (2.0 - rho * rho))

    def largest(values):
        return functools.reduce(jnp.maximum, values)

    def step(carry):
        count, rhos = carry
        after = []
        halves = [dot(system(l), inverse[l], HIGHEST) for l in range(lambda_total)]
        for l in range(lambda_total):
            rho = rhos[l]
            gain = 2.0 / (2.0 - rho * rho)
            x = inverse[l]
            inverse[l] = gain * (2.0 * x - dot(x, halves[l], HIGHEST))
            after.append(rho * rho / (2.0 - rho * rho))
        return count + 1, tuple(after)

    lax.while_loop(
        lambda carry: (largest(carry[1]) > 2e-3) & (carry[0] < 40),
        step,
        (jnp.int32(0), tuple(rhos)),
    )

    right = gram_ref[:, members:]
    firsts = [dot(inverse[l], right, HIGHEST) for l in range(lambda_total)]
    misses = [right - dot(system(l), firsts[l], HIGHEST) for l in range(lambda_total)]
    for l in range(lambda_total):
        solved = firsts[l] + dot(inverse[l], misses[l], HIGHEST)
        transform = solved.astype(BF16).astype(F32)
        if l == 0:
            centred = transform - jnp.mean(transform, axis=0, keepdims=True) + eye
            high = centred.astype(BF16)
            weights[:members, :] = high
            weights[members:, :] = (centred - high.astype(F32)).astype(BF16)
        spread = dot(cov_ref[...], transform, HIGHEST)
        norms_ref[pl.ds(l, 1), :] = jnp.sum(transform * spread, axis=0, keepdims=True)

    step_rows = rows_per_step(group_rows, 1024)
    for g in range(groups):
        group_copy(g, False).wait()

        @pl.loop(0, group_rows // step_rows)
        def _(i):
            rows = pl.ds(pl.multiple_of(g * group_rows + i * step_rows, step_rows), step_rows)
            x = field[rows, :]
            field[rows, :] = dot(jnp.concatenate([x, x], axis=1), weights[...]).astype(BF16)

        group_copy(g, True).start()
    for g in range(groups):
        group_copy(g, True).wait()


def on_device(
    log_k, heads_pred, slot_well, tile_count, obs_values, obs_std, loc_blocks, taper, lambdas
):
    n_obs = lax.axis_size("obs")
    n_cell = lax.axis_size("cell")
    total = n_obs * n_cell
    cells, members = log_k.shape
    slots = slot_well.shape[0]
    wells = obs_values.shape[0]
    band = members // n_obs
    vmem = pl.BlockSpec(memory_space=pltpu.VMEM)
    smem = pl.BlockSpec(memory_space=pltpu.SMEM)
    hbm = pl.BlockSpec(memory_space=pl.ANY)
    gram, cov = pl.pallas_call(
        functools.partial(gram_kernel, n_obs, n_cell, loc_blocks.shape[1]),
        out_shape=(
            jax.ShapeDtypeStruct((members, 2 * members), F32),
            jax.ShapeDtypeStruct((members, members), F32),
        ),
        in_specs=[vmem, vmem, smem, vmem, vmem, smem, smem, hbm],
        out_specs=(vmem, vmem),
        scratch_shapes=[
            pltpu.VMEM((cells, members), BF16),
            pltpu.VMEM((total * CAP, members), BF16),
            pltpu.VMEM((total * CAP, members), BF16),
            pltpu.VMEM((total, 1, wells), F32),
            pltpu.VMEM((total, 1, wells), F32),
            pltpu.VMEM((wells + 8, members), F32),
            pltpu.VMEM((n_cell, wells + 8, members), F32),
            pltpu.VMEM((wells, members), BF16),
            pltpu.VMEM((n_cell, wells, members), BF16),
            pltpu.VMEM((n_cell * wells, members), F32),
            pltpu.VMEM((n_cell * wells, 2 * members), F32),
            pltpu.VMEM((n_obs, band, 2 * members), F32),
            pltpu.VMEM((n_obs, band, 2 * members), F32),
            pltpu.VMEM((band, 2 * members), F32),
            pltpu.VMEM((n_obs, band, 2 * members), F32),
            pltpu.SemaphoreType.DMA((PIECES,)),
            pltpu.SemaphoreType.DMA((6,)),
            pltpu.SemaphoreType.DMA((6,)),
        ],
        compiler_params=pltpu.CompilerParams(
            collective_id=0, has_side_effects=True, vmem_limit_bytes=48 << 20
        ),
        name="gram",
    )(
        heads_pred, slot_well.reshape(1, slots), tile_count, obs_values,
        obs_std.reshape(1, wells), loc_blocks, taper, log_k,
    )
    lambda_total = lambdas.shape[0]
    groups = 12
    posterior, norms = pl.pallas_call(
        update_kernel,
        out_shape=(
            jax.ShapeDtypeStruct((cells, members), BF16),
            jax.ShapeDtypeStruct((lambda_total, members), F32),
        ),
        in_specs=[vmem, vmem, smem, hbm],
        out_specs=(hbm, vmem),
        scratch_shapes=[
            pltpu.VMEM((cells, members), BF16),
            pltpu.VMEM((lambda_total, members, members), F32),
            pltpu.VMEM((2 * members, members), BF16),
            pltpu.SemaphoreType.DMA((groups,)),
            pltpu.SemaphoreType.DMA((groups,)),
        ],
        compiler_params=pltpu.CompilerParams(vmem_limit_bytes=48 << 20),
        name="update",
    )(gram, cov, lambdas, log_k)
    return posterior, norms[None]


def solution(mesh):
    return jax.shard_map(
        on_device,
        mesh=mesh,
        in_specs=(
            P(("obs", "cell"), None),
            P(("obs", "cell"), None),
            P(("obs", "cell")),
            P(("obs", "cell")),
            P(("obs", "cell"), None),
            P(("obs", "cell")),
            P(),
            P(),
            P(),
        ),
        out_specs=(P(("obs", "cell"), None), P(("obs", "cell"), None, None)),
        check_vma=False,
    )
```

```python
import functools

import jax
import jax.numpy as jnp
from jax import lax
from jax.experimental import pallas as pl
from jax.experimental.pallas import tpu as pltpu
from jax.sharding import PartitionSpec as P

CAP = 16
PIECES = 4
MESH = pl.DeviceIdType.MESH
HIGHEST = lax.Precision.HIGHEST
F32 = jnp.float32
BF16 = jnp.bfloat16


def dot(a, b, precision=None):
    return jnp.dot(a, b, precision=precision, preferred_element_type=F32)


def dot_rows(a, b, precision=None):
    return lax.dot_general(
        a, b, (((0,), (0,)), ((), ())), precision=precision, preferred_element_type=F32
    )


def split(x):
    high = x.astype(BF16)
    rest = x - high.astype(F32)
    middle = rest.astype(BF16)
    return high, middle, (rest - middle.astype(F32)).astype(BF16)


def product(a, b):
    a_high, a_middle, a_low = split(a)
    b_high, b_middle, b_low = split(b)
    pair = jnp.concatenate([b_high, b_middle], axis=1)
    large = dot(
        jnp.concatenate([a_high, a_middle], axis=1), jnp.concatenate([pair, pair], axis=0)
    )
    small = dot(
        jnp.concatenate([a_low, a_high], axis=1), jnp.concatenate([b_high, b_low], axis=0)
    )
    columns = b.shape[1]
    return large[:, :columns] + (large[:, columns:] + small)


def divide(x, n):
    if n & (n - 1) == 0:
        return lax.shift_right_logical(x, jnp.full(x.shape, n.bit_length() - 1, x.dtype))
    return x // n


def rows_per_step(total, most):
    step = most
    while total % step:
        step //= 2
    return step


def gram_kernel(
    n_obs, n_cell,
    heads_in, well_in, count_in, obs_in, std_in, loc_in, taper_in, log_k_ref,
    gram_ref, cov_ref,
    heads_ref, well_ref, count_ref, std_ref, loc_ref, taper_ref, in_sem, field, send_heads, recv_heads, send_idx, recv_idx, obs_send, obs_all, pred_send, pred_all,
    s_all, d_all, part, bands, band_sum, summed, field_sem, send_sem, recv_sem,
):
    total = n_obs * n_cell
    o, c = lax.axis_index("obs"), lax.axis_index("cell")
    me = o * n_cell + c
    cells, members = field.shape
    wells = obs_in.shape[0]
    slots = heads_ref.shape[0]
    piece_rows = cells // PIECES

    def piece_copy(p):
        rows = pl.ds(p * piece_rows, piece_rows)
        return pltpu.make_async_copy(log_k_ref.at[rows], field.at[rows], field_sem.at[p])

    inputs = [
        pltpu.make_async_copy(src, dst, in_sem.at[i])
        for i, (src, dst) in enumerate((
            (well_in, well_ref), (count_in, count_ref), (heads_in, heads_ref),
            (std_in, std_ref), (loc_in, loc_ref), (taper_in, taper_ref),
            (obs_in, obs_send.at[pl.ds(0, wells)]),
        ))
    ]
    for copy in inputs:
        copy.start()
    for p in range(PIECES):
        piece_copy(p).start()

    barrier = pltpu.get_barrier_semaphore()

    @pl.loop(1, total)
    def _(i):
        to = lax.rem(me + i, total)
        pl.semaphore_signal(
            barrier, inc=1, device_id=(to // n_cell, lax.rem(to, n_cell)), device_id_type=MESH
        )

    for copy in inputs:
        copy.wait()

    well = well_ref[...]
    lane = lax.broadcasted_iota(jnp.int32, (1, slots), 1)
    owner = divide(well, wells)
    place_in = (well - owner * wells + 1).astype(F32)
    owner = jnp.where(lane < count_ref[0], owner, total)
    lane_f = lane.astype(F32)
    group = 8
    rows_now = group * CAP
    row_at = lax.broadcasted_iota(jnp.int32, (rows_now, 1), 0)
    in_group = divide(row_at, CAP)
    rank = (row_at - in_group * CAP).astype(F32)
    well_lane = lax.broadcasted_iota(jnp.int32, (1, wells), 1).astype(F32)

    @pl.loop(0, total // group)
    def _(i):
        dest = in_group + i * group
        start = jnp.sum(jnp.where(owner < dest, 1.0, 0.0), axis=1, keepdims=True)
        hit = jnp.where((owner == dest) & (lane_f == start + rank), 1.0, 0.0)
        rows = pl.ds(pl.multiple_of(i * rows_now, rows_now), rows_now)
        send_heads[rows, :] = dot(hit.astype(BF16), heads_ref[...]).astype(BF16)
        place = jnp.sum(hit * place_in, axis=1, keepdims=True) - 1.0
        ranks = jnp.where(place == well_lane, rank + 1.0, 0.0)
        for q in range(group):
            send_idx[i * group + q] = (
                jnp.sum(ranks[q * CAP : (q + 1) * CAP], axis=0, keepdims=True) - 1.0
            )

    obs_send[wells:, :] = jnp.broadcast_to(std_ref[...], (8, wells))
    pl.semaphore_wait(barrier, total - 1)

    def head_rows(d):
        return pl.ds(pl.multiple_of(d * CAP, CAP), CAP)

    @pl.loop(1, total)
    def _(i):
        to = lax.rem(me + i, total)
        device = (to // n_cell, lax.rem(to, n_cell))
        pltpu.make_async_remote_copy(
            src_ref=send_heads.at[head_rows(to)], dst_ref=recv_heads.at[head_rows(me)],
            send_sem=send_sem.at[0], recv_sem=recv_sem.at[0],
            device_id=device, device_id_type=MESH,
        ).start()
        pltpu.make_async_remote_copy(
            src_ref=send_idx.at[to], dst_ref=recv_idx.at[me],
            send_sem=send_sem.at[1], recv_sem=recv_sem.at[1],
            device_id=device, device_id_type=MESH,
        ).start()

    pltpu.make_async_copy(
        send_heads.at[head_rows(me)], recv_heads.at[head_rows(me)], recv_sem.at[0]
    ).start()
    pltpu.make_async_copy(send_idx.at[me], recv_idx.at[me], recv_sem.at[1]).start()

    def to_cells(src, dst, at):
        @pl.loop(1, n_cell)
        def _(i):
            pltpu.make_async_remote_copy(
                src_ref=src, dst_ref=dst.at[c], send_sem=send_sem.at[at],
                recv_sem=recv_sem.at[at],
                device_id=(o, lax.rem(c + i, n_cell)), device_id_type=MESH,
            ).start()

        pltpu.make_async_copy(src, dst.at[c], recv_sem.at[at]).start()

    to_cells(obs_send, obs_all, 2)

    wide = (2 * members, 2 * members)
    at_row = lax.broadcasted_iota(jnp.int32, wide, 0)
    at_column = lax.broadcasted_iota(jnp.int32, wide, 1)
    centring = jnp.where(at_row == at_column, 1.0, 0.0) - jnp.where(
        (at_row < members) == (at_column < members), 1.0 / members, 0.0
    )
    centring = centring.astype(BF16)
    step_rows = rows_per_step(piece_rows, 2048)
    half_rows = step_rows // 2
    cov_ref[...] = jnp.zeros_like(cov_ref)

    def covariance(p):
        piece_copy(p).wait()

        @pl.loop(0, piece_rows // step_rows)
        def _(i):
            at = pl.multiple_of(p * piece_rows + i * step_rows, step_rows)
            x = jnp.concatenate(
                [field[pl.ds(at, half_rows), :], field[pl.ds(at + half_rows, half_rows), :]],
                axis=1,
            )
            anomalies = dot(x, centring).astype(BF16)
            left, right = anomalies[:, :members], anomalies[:, members:]
            cov_ref[...] += dot_rows(left, left) + dot_rows(right, right)

    def arrived(ref, at):
        pltpu.make_async_copy(ref, ref, recv_sem.at[at]).wait()

    covariance(0)
    arrived(recv_heads, 0)
    arrived(recv_idx, 1)
    ranks_at = lax.broadcasted_iota(jnp.int32, (total, CAP, wells), 1).astype(F32)
    take = jnp.where(recv_idx[...] == ranks_at, 1.0, 0.0).reshape(total * CAP, wells)
    pred_send[...] = dot_rows(take.astype(BF16), recv_heads[...]).astype(BF16)
    to_cells(pred_send, pred_all, 3)

    covariance(1)
    arrived(obs_all, 2)
    arrived(pred_all, 3)
    eye = (
        lax.broadcasted_iota(jnp.int32, (wells, wells), 0)
        == lax.broadcasted_iota(jnp.int32, (wells, wells), 1)
    )

    @pl.loop(0, n_cell)
    def _(b):
        block = o * n_cell + b
        weight = jnp.sum(
            jnp.where(loc_ref[pl.ds(c, 1), :] == block, taper_ref[pl.ds(c, 1), :], 0.0),
            axis=1, keepdims=True,
        )
        std = jnp.sum(
            jnp.where(eye, obs_all[b, pl.ds(wells, 1), :], 0.0), axis=1, keepdims=True
        )
        inverse = 1.0 / std
        pred = pred_all[b].astype(F32)
        mean = jnp.mean(pred, axis=1, keepdims=True)
        scaled = (pred - mean) * inverse
        rows = pl.ds(pl.multiple_of(b * wells, wells), wells)
        s_all[rows, :] = scaled * weight
        d_all[rows, :members] = scaled
        d_all[rows, members:] = (obs_all[b, pl.ds(0, wells), :] - pred) * inverse

    product = dot_rows(s_all[...], d_all[...], HIGHEST)
    band = members // n_obs
    part[...] = product.reshape(part.shape)

    def obs_copies(src_of, dst, at):
        @pl.loop(1, n_obs)
        def _(i):
            to = lax.rem(o + i, n_obs)
            pltpu.make_async_remote_copy(
                src_ref=src_of(to), dst_ref=dst.at[o], send_sem=send_sem.at[at],
                recv_sem=recv_sem.at[at], device_id=(to, c), device_id_type=MESH,
            ).start()

        pltpu.make_async_copy(src_of(o), dst.at[o], recv_sem.at[at]).start()

    obs_copies(lambda to: part.at[to], bands, 4)
    covariance(2)
    arrived(bands, 4)
    band_sum[...] = jnp.sum(bands[...], axis=0)
    obs_copies(lambda to: band_sum, summed, 5)
    covariance(3)
    arrived(summed, 5)
    gram_ref[...] = summed[...].reshape(gram_ref.shape)

    def sent(ref, at):
        pltpu.make_async_copy(ref, ref, send_sem.at[at]).wait()

    sent(recv_heads.at[pl.ds(0, (total - 1) * CAP)], 0)
    sent(recv_idx.at[pl.ds(0, total - 1)], 1)
    sent(obs_all.at[pl.ds(0, n_cell - 1)], 2)
    sent(pred_all.at[pl.ds(0, n_cell - 1)], 3)
    sent(bands.at[pl.ds(0, n_obs - 1)], 4)
    sent(summed.at[pl.ds(0, n_obs - 1)], 5)


def update_kernel(
    gram_ref, cov_ref, lambda_ref, log_k_ref, posterior_ref, norms_ref,
    field, inverse, weights, in_sem, out_sem,
):
    cells, members = field.shape
    groups = in_sem.shape[0]
    group_rows = cells // groups
    lambda_total = lambda_ref.shape[0]

    def group_copy(g, back):
        rows = pl.ds(g * group_rows, group_rows)
        if back:
            return pltpu.make_async_copy(field.at[rows], posterior_ref.at[rows], out_sem.at[g])
        return pltpu.make_async_copy(log_k_ref.at[rows], field.at[rows], in_sem.at[g])

    for g in range(groups):
        group_copy(g, False).start()

    curvature = gram_ref[:, :members]
    square = product(curvature, curvature)
    top = jnp.sqrt(jnp.max(jnp.sum(jnp.abs(square), axis=1, keepdims=True)))
    top = jnp.minimum(top, jnp.max(jnp.sum(jnp.abs(curvature), axis=1, keepdims=True)))
    cube = product(square, curvature)
    eye = jnp.where(
        lax.broadcasted_iota(jnp.int32, (members, members), 0)
        == lax.broadcasted_iota(jnp.int32, (members, members), 1),
        1.0, 0.0,
    )
    shifts = [(1.0 + lambda_ref[l]) * (members - 1) for l in range(lambda_total)]

    def advance(rho):
        return 2.0 / (2.0 - rho * rho), rho * rho / (2.0 - rho * rho)

    def block(l):
        return pl.ds(l * members, members)

    rhos = []
    for l in range(lambda_total):
        shift = shifts[l]
        first = 2.0 / (2.0 * shift + top)
        gain, rho = advance(top * (0.5 * first))
        u, v = 2.0 * gain * first, gain * first * first
        gain, rho = advance(rho)
        terms = (
            2.0 * u - 2.0 * v * shift - shift * (u - v * shift) * (u - v * shift),
            -2.0 * v - (u - v * shift) * (u - 3.0 * v * shift),
            v * (2.0 * u - 3.0 * v * shift),
            -v * v,
        )
        inverse[block(l), :] = gain * (
            terms[0] * eye + terms[1] * curvature + terms[2] * square + terms[3] * cube
        )
        rhos.append(rho)

    def largest(values):
        return functools.reduce(jnp.maximum, values)

    def step(carry):
        count, rhos = carry
        after = []
        shared = product(inverse[...], gram_ref[:, :members])
        for l in range(lambda_total):
            gain, rho = advance(rhos[l])
            x = inverse[block(l), :]
            half = shared[l * members : (l + 1) * members] + shifts[l] * x
            inverse[block(l), :] = gain * (2.0 * x - product(half, x))
            after.append(rho)
        return count + 1, tuple(after)

    lax.while_loop(
        lambda carry: (largest(carry[1]) > 3e-5) & (carry[0] < 40),
        step,
        (jnp.int32(0), tuple(rhos)),
    )

    solved = product(inverse[...], gram_ref[:, members:]).astype(BF16)
    transform = solved[:members].astype(F32)
    centred = transform - jnp.mean(transform, axis=0, keepdims=True) + eye
    high = centred.astype(BF16)
    weights[:members, :] = high
    weights[members:, :] = (centred - high.astype(F32)).astype(BF16)

    step_rows = rows_per_step(group_rows, 1024)
    for g in range(groups):
        group_copy(g, False).wait()

        @pl.loop(0, group_rows // step_rows)
        def _(i):
            rows = pl.ds(pl.multiple_of(g * group_rows + i * step_rows, step_rows), step_rows)
            x = field[rows, :]
            field[rows, :] = dot(jnp.concatenate([x, x], axis=1), weights[...]).astype(BF16)

        group_copy(g, True).start()

    beside = jnp.concatenate(
        [solved[l * members : (l + 1) * members] for l in range(lambda_total)], axis=1
    )
    high, middle, low = split(cov_ref[...])
    spread = dot(
        jnp.concatenate([high, middle], axis=1), jnp.concatenate([beside, beside], axis=0)
    ) + dot(low, beside)
    norms = jnp.sum(beside.astype(F32) * spread, axis=0, keepdims=True)
    for l in range(lambda_total):
        norms_ref[pl.ds(l, 1), :] = norms[:, l * members : (l + 1) * members]
    for g in range(groups):
        group_copy(g, True).wait()


def on_device(
    log_k, heads_pred, slot_well, tile_count, obs_values, obs_std, loc_blocks, taper, lambdas
):
    n_obs = lax.axis_size("obs")
    n_cell = lax.axis_size("cell")
    total = n_obs * n_cell
    cells, members = log_k.shape
    slots = slot_well.shape[0]
    wells = obs_values.shape[0]
    band = members // n_obs
    vmem = pl.BlockSpec(memory_space=pltpu.VMEM)
    smem = pl.BlockSpec(memory_space=pltpu.SMEM)
    hbm = pl.BlockSpec(memory_space=pl.ANY)
    gram, cov = pl.pallas_call(
        functools.partial(gram_kernel, n_obs, n_cell),
        out_shape=(
            jax.ShapeDtypeStruct((members, 2 * members), F32),
            jax.ShapeDtypeStruct((members, members), F32),
        ),
        in_specs=[hbm] * 8,
        out_specs=(vmem, vmem),
        scratch_shapes=[
            pltpu.VMEM((slots, members), BF16),
            pltpu.VMEM((1, slots), jnp.int32),
            pltpu.SMEM((1,), jnp.int32),
            pltpu.VMEM((1, wells), F32),
            pltpu.VMEM(loc_blocks.shape, jnp.int32),
            pltpu.VMEM(taper.shape, F32),
            pltpu.SemaphoreType.DMA((7,)),
            pltpu.VMEM((cells, members), BF16),
            pltpu.VMEM((total * CAP, members), BF16),
            pltpu.VMEM((total * CAP, members), BF16),
            pltpu.VMEM((total, 1, wells), F32),
            pltpu.VMEM((total, 1, wells), F32),
            pltpu.VMEM((wells + 8, members), F32),
            pltpu.VMEM((n_cell, wells + 8, members), F32),
            pltpu.VMEM((wells, members), BF16),
            pltpu.VMEM((n_cell, wells, members), BF16),
            pltpu.VMEM((n_cell * wells, members), F32),
            pltpu.VMEM((n_cell * wells, 2 * members), F32),
            pltpu.VMEM((n_obs, band, 2 * members), F32),
            pltpu.VMEM((n_obs, band, 2 * members), F32),
            pltpu.VMEM((band, 2 * members), F32),
            pltpu.VMEM((n_obs, band, 2 * members), F32),
            pltpu.SemaphoreType.DMA((PIECES,)),
            pltpu.SemaphoreType.DMA((6,)),
            pltpu.SemaphoreType.DMA((6,)),
        ],
        compiler_params=pltpu.CompilerParams(
            collective_id=0, has_side_effects=True, vmem_limit_bytes=60 << 20
        ),
        name="gram",
    )(
        heads_pred, slot_well.reshape(1, slots), tile_count, obs_values,
        obs_std.reshape(1, wells), loc_blocks, taper, log_k,
    )
    lambda_total = lambdas.shape[0]
    groups = 12
    posterior, norms = pl.pallas_call(
        update_kernel,
        out_shape=(
            jax.ShapeDtypeStruct((cells, members), BF16),
            jax.ShapeDtypeStruct((lambda_total, members), F32),
        ),
        in_specs=[vmem, vmem, smem, hbm],
        out_specs=(hbm, vmem),
        scratch_shapes=[
            pltpu.VMEM((cells, members), BF16),
            pltpu.VMEM((lambda_total * members, members), F32),
            pltpu.VMEM((2 * members, members), BF16),
            pltpu.SemaphoreType.DMA((groups,)),
            pltpu.SemaphoreType.DMA((groups,)),
        ],
        compiler_params=pltpu.CompilerParams(vmem_limit_bytes=60 << 20),
        name="update",
    )(gram, cov, lambdas, log_k)
    return posterior, norms[None]


def solution(mesh):
    return jax.shard_map(
        on_device,
        mesh=mesh,
        in_specs=(
            P(("obs", "cell"), None),
            P(("obs", "cell"), None),
            P(("obs", "cell")),
            P(("obs", "cell")),
            P(("obs", "cell"), None),
            P(("obs", "cell")),
            P(),
            P(),
            P(),
        ),
        out_specs=(P(("obs", "cell"), None), P(("obs", "cell"), None, None)),
        check_vma=False,
    )
```

```python
import functools

import jax
import jax.numpy as jnp
from jax import lax
from jax.experimental import pallas as pl
from jax.experimental.pallas import tpu as pltpu
from jax.sharding import PartitionSpec as P

CAP = 16
PIECES = 6
MESH = pl.DeviceIdType.MESH
HIGHEST = lax.Precision.HIGHEST
F32 = jnp.float32
BF16 = jnp.bfloat16


def dot(a, b, precision=None):
    return jnp.dot(a, b, precision=precision, preferred_element_type=F32)


def dot_rows(a, b, precision=None):
    return lax.dot_general(
        a, b, (((0,), (0,)), ((), ())), precision=precision, preferred_element_type=F32
    )


def split(x):
    high = x.astype(BF16)
    rest = x - high.astype(F32)
    middle = rest.astype(BF16)
    return high, middle, (rest - middle.astype(F32)).astype(BF16)


def product(a, b):
    a_high, a_middle, a_low = split(a)
    b_high, b_middle, b_low = split(b)
    pair = jnp.concatenate([b_high, b_middle], axis=1)
    large = dot(
        jnp.concatenate([a_high, a_middle], axis=1), jnp.concatenate([pair, pair], axis=0)
    )
    small = dot(
        jnp.concatenate([a_low, a_high], axis=1), jnp.concatenate([b_high, b_low], axis=0)
    )
    columns = b.shape[1]
    return large[:, :columns] + (large[:, columns:] + small)


def divide(x, n):
    if n & (n - 1) == 0:
        return lax.shift_right_logical(x, jnp.full(x.shape, n.bit_length() - 1, x.dtype))
    return x // n


def rows_per_step(total, most):
    step = most
    while total % step:
        step //= 2
    return step


def gram_kernel(
    n_obs, n_cell,
    heads_in, well_in, count_in, obs_in, std_in, loc_in, taper_in, log_k_ref,
    gram_ref, cov_ref,
    heads_ref, well_ref, count_ref, std_ref, loc_ref, taper_ref, in_sem, field, squares,
    send_heads, mid_heads, recv_heads, send_idx, mid_idx, recv_idx,
    obs_send, obs_all, pred_send, pred_all, s_all, d_all, part, bands, band_sum, summed, field_sem, send_sem, recv_sem,
):
    total = n_obs * n_cell
    o, c = lax.axis_index("obs"), lax.axis_index("cell")
    cells, members = field.shape
    wells = obs_in.shape[0]
    slots = heads_ref.shape[0]
    piece_rows = cells // PIECES

    def piece_copy(p):
        rows = pl.ds(p * piece_rows, piece_rows)
        return pltpu.make_async_copy(log_k_ref.at[rows], field.at[rows], field_sem.at[p])

    inputs = [
        pltpu.make_async_copy(src, dst, in_sem.at[i])
        for i, (src, dst) in enumerate((
            (well_in, well_ref), (count_in, count_ref), (heads_in, heads_ref),
            (std_in, std_ref), (loc_in, loc_ref), (taper_in, taper_ref),
            (obs_in, obs_send.at[pl.ds(0, wells)]),
        ))
    ]
    for copy in inputs:
        copy.start()
    for p in range(PIECES):
        piece_copy(p).start()

    barrier = pltpu.get_barrier_semaphore()

    @pl.loop(1, n_obs)
    def _(i):
        pl.semaphore_signal(
            barrier, inc=1, device_id=(lax.rem(o + i, n_obs), c), device_id_type=MESH
        )

    @pl.loop(1, n_cell)
    def _(i):
        pl.semaphore_signal(
            barrier, inc=1, device_id=(o, lax.rem(c + i, n_cell)), device_id_type=MESH
        )

    for copy in inputs:
        copy.wait()

    well = well_ref[...]
    lane = lax.broadcasted_iota(jnp.int32, (1, slots), 1)
    owner = divide(well, wells)
    place_in = (well - owner * wells + 1).astype(F32)
    owner = jnp.where(lane < count_ref[0], owner, total)
    lane_f = lane.astype(F32)
    group = 8
    rows_now = group * CAP
    row_at = lax.broadcasted_iota(jnp.int32, (rows_now, 1), 0)
    in_group = divide(row_at, CAP)
    rank = (row_at - in_group * CAP).astype(F32)
    well_lane = lax.broadcasted_iota(jnp.int32, (1, wells), 1).astype(F32)

    @pl.loop(0, total // group)
    def _(i):
        dest = in_group + i * group
        start = jnp.sum(jnp.where(owner < dest, 1.0, 0.0), axis=1, keepdims=True)
        hit = jnp.where((owner == dest) & (lane_f == start + rank), 1.0, 0.0)
        rows = pl.ds(pl.multiple_of(i * rows_now, rows_now), rows_now)
        send_heads[rows, :] = dot(hit.astype(BF16), heads_ref[...]).astype(BF16)
        place = jnp.sum(hit * place_in, axis=1, keepdims=True) - 1.0
        ranks = jnp.where(place == well_lane, rank + 1.0, 0.0)
        for q in range(group):
            send_idx[i * group + q] = (
                jnp.sum(ranks[q * CAP : (q + 1) * CAP], axis=0, keepdims=True) - 1.0
            )

    obs_send[wells:, :] = jnp.broadcast_to(std_ref[...], (8, wells))
    pl.semaphore_wait(barrier, n_obs + n_cell - 2)

    def to_obs(src_of, dst, at):
        @pl.loop(1, n_obs)
        def _(i):
            to = lax.rem(o + i, n_obs)
            pltpu.make_async_remote_copy(
                src_ref=src_of(to), dst_ref=dst.at[o], send_sem=send_sem.at[at],
                recv_sem=recv_sem.at[at], device_id=(to, c), device_id_type=MESH,
            ).start()

        pltpu.make_async_copy(src_of(o), dst.at[o], recv_sem.at[at]).start()

    def to_cells(src_of, dst, at):
        @pl.loop(1, n_cell)
        def _(i):
            to = lax.rem(c + i, n_cell)
            pltpu.make_async_remote_copy(
                src_ref=src_of(to), dst_ref=dst.at[c], send_sem=send_sem.at[at],
                recv_sem=recv_sem.at[at], device_id=(o, to), device_id_type=MESH,
            ).start()

        pltpu.make_async_copy(src_of(c), dst.at[c], recv_sem.at[at]).start()

    line = n_cell * CAP
    to_obs(lambda to: send_heads.at[pl.ds(pl.multiple_of(to * line, line), line)], mid_heads, 0)
    to_obs(lambda to: send_idx.at[pl.ds(to * n_cell, n_cell)], mid_idx, 1)
    to_cells(lambda to: obs_send, obs_all, 2)

    wide = (2 * members, 2 * members)
    at_row = lax.broadcasted_iota(jnp.int32, wide, 0)
    at_column = lax.broadcasted_iota(jnp.int32, wide, 1)
    centring = jnp.where(at_row == at_column, 1.0, 0.0) - jnp.where(
        (at_row < members) == (at_column < members), 1.0 / members, 0.0
    )
    centring = centring.astype(BF16)
    step_rows = rows_per_step(piece_rows, 2048)
    half_rows = step_rows // 2
    squares[...] = jnp.zeros_like(squares)

    def covariance(p):
        piece_copy(p).wait()

        @pl.loop(0, piece_rows // step_rows)
        def _(i):
            at = pl.multiple_of(p * piece_rows + i * step_rows, step_rows)
            x = jnp.concatenate(
                [field[pl.ds(at, half_rows), :], field[pl.ds(at + half_rows, half_rows), :]],
                axis=1,
            )
            anomalies = dot(x, centring).astype(BF16)
            squares[...] += dot_rows(anomalies, anomalies)

    def arrived(ref, at):
        pltpu.make_async_copy(ref, ref, recv_sem.at[at]).wait()

    covariance(0)
    arrived(mid_heads, 0)
    arrived(mid_idx, 1)
    to_cells(lambda to: mid_heads.at[:, pl.ds(pl.multiple_of(to * CAP, CAP), CAP)], recv_heads, 6)
    to_cells(lambda to: mid_idx.at[:, to], recv_idx, 7)
    covariance(1)
    arrived(recv_heads, 6)
    arrived(recv_idx, 7)
    ranks_at = lax.broadcasted_iota(jnp.int32, (total, CAP, wells), 1).astype(F32)
    ranks = recv_idx[...].reshape(total, 1, wells)
    take = jnp.where(ranks == ranks_at, 1.0, 0.0).reshape(total * CAP, wells)
    heads = recv_heads[...].reshape(total * CAP, members)
    pred_send[...] = dot_rows(take.astype(BF16), heads).astype(BF16)
    to_cells(lambda to: pred_send, pred_all, 3)

    covariance(2)
    covariance(3)
    arrived(obs_all, 2)
    arrived(pred_all, 3)
    eye = (
        lax.broadcasted_iota(jnp.int32, (wells, wells), 0)
        == lax.broadcasted_iota(jnp.int32, (wells, wells), 1)
    )

    @pl.loop(0, n_cell)
    def _(b):
        block = o * n_cell + b
        weight = jnp.sum(
            jnp.where(loc_ref[pl.ds(c, 1), :] == block, taper_ref[pl.ds(c, 1), :], 0.0),
            axis=1, keepdims=True,
        )
        std = jnp.sum(
            jnp.where(eye, obs_all[b, pl.ds(wells, 1), :], 0.0), axis=1, keepdims=True
        )
        inverse = 1.0 / std
        pred = pred_all[b].astype(F32)
        mean = jnp.mean(pred, axis=1, keepdims=True)
        scaled = (pred - mean) * inverse
        rows = pl.ds(pl.multiple_of(b * wells, wells), wells)
        s_all[rows, :] = scaled * weight
        d_all[rows, :members] = scaled
        d_all[rows, members:] = (obs_all[b, pl.ds(0, wells), :] - pred) * inverse

    product = dot_rows(s_all[...], d_all[...], HIGHEST)
    band = members // n_obs
    part[...] = product.reshape(part.shape)

    to_obs(lambda to: part.at[to], bands, 4)
    covariance(4)
    arrived(bands, 4)
    band_sum[...] = jnp.sum(bands[...], axis=0)
    to_obs(lambda to: band_sum, summed, 5)
    covariance(5)
    arrived(summed, 5)
    gram_ref[...] = summed[...].reshape(gram_ref.shape)
    cov_ref[...] = squares[:members, :members] + squares[members:, members:]

    def sent(ref, at):
        pltpu.make_async_copy(ref, ref, send_sem.at[at]).wait()

    sent(mid_heads.at[pl.ds(0, n_obs - 1)], 0)
    sent(mid_idx.at[pl.ds(0, n_obs - 1)], 1)
    sent(recv_heads.at[pl.ds(0, n_cell - 1)], 6)
    sent(recv_idx.at[pl.ds(0, n_cell - 1)], 7)
    sent(obs_all.at[pl.ds(0, n_cell - 1)], 2)
    sent(pred_all.at[pl.ds(0, n_cell - 1)], 3)
    sent(bands.at[pl.ds(0, n_obs - 1)], 4)
    sent(summed.at[pl.ds(0, n_obs - 1)], 5)


def update_kernel(
    gram_ref, cov_ref, lambda_ref, log_k_ref, posterior_ref, norms_ref,
    field, inverse, weights, in_sem, out_sem,
):
    cells, members = field.shape
    groups = in_sem.shape[0]
    group_rows = cells // groups
    lambda_total = lambda_ref.shape[0]

    def group_copy(g, back):
        rows = pl.ds(g * group_rows, group_rows)
        if back:
            return pltpu.make_async_copy(field.at[rows], posterior_ref.at[rows], out_sem.at[g])
        return pltpu.make_async_copy(log_k_ref.at[rows], field.at[rows], in_sem.at[g])

    for g in range(groups):
        group_copy(g, False).start()

    curvature = gram_ref[:, :members]
    square = product(curvature, curvature)
    top = jnp.sqrt(jnp.max(jnp.sum(jnp.abs(square), axis=1, keepdims=True)))
    top = jnp.minimum(top, jnp.max(jnp.sum(jnp.abs(curvature), axis=1, keepdims=True)))
    cube = product(square, curvature)
    eye = jnp.where(
        lax.broadcasted_iota(jnp.int32, (members, members), 0)
        == lax.broadcasted_iota(jnp.int32, (members, members), 1),
        1.0, 0.0,
    )
    shifts = [(1.0 + lambda_ref[l]) * (members - 1) for l in range(lambda_total)]

    def advance(rho):
        return 2.0 / (2.0 - rho * rho), rho * rho / (2.0 - rho * rho)

    def block(l):
        return pl.ds(l * members, members)

    rhos = []
    for l in range(lambda_total):
        shift = shifts[l]
        first = 2.0 / (2.0 * shift + top)
        gain, rho = advance(top * (0.5 * first))
        u, v = 2.0 * gain * first, gain * first * first
        gain, rho = advance(rho)
        terms = (
            2.0 * u - 2.0 * v * shift - shift * (u - v * shift) * (u - v * shift),
            -2.0 * v - (u - v * shift) * (u - 3.0 * v * shift),
            v * (2.0 * u - 3.0 * v * shift),
            -v * v,
        )
        inverse[block(l), :] = gain * (
            terms[0] * eye + terms[1] * curvature + terms[2] * square + terms[3] * cube
        )
        rhos.append(rho)

    def largest(values):
        return functools.reduce(jnp.maximum, values)

    def step(carry):
        count, rhos = carry
        after = []
        shared = product(inverse[...], gram_ref[:, :members])
        for l in range(lambda_total):
            gain, rho = advance(rhos[l])
            x = inverse[block(l), :]
            half = shared[l * members : (l + 1) * members] + shifts[l] * x
            inverse[block(l), :] = gain * (2.0 * x - product(half, x))
            after.append(rho)
        return count + 1, tuple(after)

    lax.while_loop(
        lambda carry: (largest(carry[1]) > 3e-5) & (carry[0] < 40),
        step,
        (jnp.int32(0), tuple(rhos)),
    )

    solved = product(inverse[...], gram_ref[:, members:]).astype(BF16)
    transform = solved[:members].astype(F32)
    centred = transform - jnp.mean(transform, axis=0, keepdims=True) + eye
    high = centred.astype(BF16)
    low = (centred - high.astype(F32)).astype(BF16)
    none = jnp.zeros_like(high)
    weights[:members, :] = jnp.concatenate([high, none, low, none], axis=1)
    weights[members:, :] = jnp.concatenate([none, high, none, low], axis=1)

    step_rows = rows_per_step(group_rows, 2048)
    half_rows = step_rows // 2
    for g in range(groups):
        group_copy(g, False).wait()

        @pl.loop(0, group_rows // step_rows)
        def _(i):
            at = pl.multiple_of(g * group_rows + i * step_rows, step_rows)
            upper, lower = pl.ds(at, half_rows), pl.ds(at + half_rows, half_rows)
            x = jnp.concatenate([field[upper, :], field[lower, :]], axis=1)
            both = dot(x, weights[...])
            both = (both[:, : 2 * members] + both[:, 2 * members :]).astype(BF16)
            field[upper, :] = both[:, :members]
            field[lower, :] = both[:, members:]

        group_copy(g, True).start()

    beside = jnp.concatenate(
        [solved[l * members : (l + 1) * members] for l in range(lambda_total)], axis=1
    )
    high, middle, low = split(cov_ref[...])
    spread = dot(
        jnp.concatenate([high, middle], axis=1), jnp.concatenate([beside, beside], axis=0)
    ) + dot(low, beside)
    norms = jnp.sum(beside.astype(F32) * spread, axis=0, keepdims=True)
    for l in range(lambda_total):
        norms_ref[pl.ds(l, 1), :] = norms[:, l * members : (l + 1) * members]
    for g in range(groups):
        group_copy(g, True).wait()


def on_device(
    log_k, heads_pred, slot_well, tile_count, obs_values, obs_std, loc_blocks, taper, lambdas
):
    n_obs = lax.axis_size("obs")
    n_cell = lax.axis_size("cell")
    total = n_obs * n_cell
    cells, members = log_k.shape
    slots = slot_well.shape[0]
    wells = obs_values.shape[0]
    band = members // n_obs
    vmem = pl.BlockSpec(memory_space=pltpu.VMEM)
    smem = pl.BlockSpec(memory_space=pltpu.SMEM)
    hbm = pl.BlockSpec(memory_space=pl.ANY)
    gram, cov = pl.pallas_call(
        functools.partial(gram_kernel, n_obs, n_cell),
        out_shape=(
            jax.ShapeDtypeStruct((members, 2 * members), F32),
            jax.ShapeDtypeStruct((members, members), F32),
        ),
        in_specs=[hbm] * 8,
        out_specs=(vmem, vmem),
        scratch_shapes=[
            pltpu.VMEM((slots, members), BF16),
            pltpu.VMEM((1, slots), jnp.int32),
            pltpu.SMEM((1,), jnp.int32),
            pltpu.VMEM((1, wells), F32),
            pltpu.VMEM(loc_blocks.shape, jnp.int32),
            pltpu.VMEM(taper.shape, F32),
            pltpu.SemaphoreType.DMA((7,)),
            pltpu.VMEM((cells, members), BF16),
            pltpu.VMEM((2 * members, 2 * members), F32),
            pltpu.VMEM((total * CAP, members), BF16),
            pltpu.VMEM((n_obs, n_cell * CAP, members), BF16),
            pltpu.VMEM((n_cell, n_obs, CAP, members), BF16),
            pltpu.VMEM((total, 1, wells), F32),
            pltpu.VMEM((n_obs, n_cell, 1, wells), F32),
            pltpu.VMEM((n_cell, n_obs, 1, wells), F32),
            pltpu.VMEM((wells + 8, members), F32),
            pltpu.VMEM((n_cell, wells + 8, members), F32),
            pltpu.VMEM((wells, members), BF16),
            pltpu.VMEM((n_cell, wells, members), BF16),
            pltpu.VMEM((n_cell * wells, members), F32),
            pltpu.VMEM((n_cell * wells, 2 * members), F32),
            pltpu.VMEM((n_obs, band, 2 * members), F32),
            pltpu.VMEM((n_obs, band, 2 * members), F32),
            pltpu.VMEM((band, 2 * members), F32),
            pltpu.VMEM((n_obs, band, 2 * members), F32),
            pltpu.SemaphoreType.DMA((PIECES,)),
            pltpu.SemaphoreType.DMA((8,)),
            pltpu.SemaphoreType.DMA((8,)),
        ],
        compiler_params=pltpu.CompilerParams(
            collective_id=0, has_side_effects=True, vmem_limit_bytes=60 << 20
        ),
        name="gram",
    )(
        heads_pred, slot_well.reshape(1, slots), tile_count, obs_values,
        obs_std.reshape(1, wells), loc_blocks, taper, log_k,
    )
    lambda_total = lambdas.shape[0]
    groups = 12
    posterior, norms = pl.pallas_call(
        update_kernel,
        out_shape=(
            jax.ShapeDtypeStruct((cells, members), BF16),
            jax.ShapeDtypeStruct((lambda_total, members), F32),
        ),
        in_specs=[vmem, vmem, smem, hbm],
        out_specs=(hbm, vmem),
        scratch_shapes=[
            pltpu.VMEM((cells, members), BF16),
            pltpu.VMEM((lambda_total * members, members), F32),
            pltpu.VMEM((2 * members, 4 * members), BF16),
            pltpu.SemaphoreType.DMA((groups,)),
            pltpu.SemaphoreType.DMA((groups,)),
        ],
        compiler_params=pltpu.CompilerParams(vmem_limit_bytes=60 << 20),
        name="update",
    )(gram, cov, lambdas, log_k)
    return posterior, norms[None]


def solution(mesh):
    return jax.shard_map(
        on_device,
        mesh=mesh,
        in_specs=(
            P(("obs", "cell"), None),
            P(("obs", "cell"), None),
            P(("obs", "cell")),
            P(("obs", "cell")),
            P(("obs", "cell"), None),
            P(("obs", "cell")),
            P(),
            P(),
            P(),
        ),
        out_specs=(P(("obs", "cell"), None), P(("obs", "cell"), None, None)),
        check_vma=False,
    )
```

```python
import functools

import jax
import jax.numpy as jnp
from jax import lax
from jax.experimental import pallas as pl
from jax.experimental.pallas import tpu as pltpu
from jax.sharding import PartitionSpec as P

CAP = 16
PIECES = 6
MESH = pl.DeviceIdType.MESH
HIGHEST = lax.Precision.HIGHEST
F32 = jnp.float32
BF16 = jnp.bfloat16


def dot(a, b, precision=None):
    return jnp.dot(a, b, precision=precision, preferred_element_type=F32)


def dot_rows(a, b, precision=None):
    return lax.dot_general(
        a, b, (((0,), (0,)), ((), ())), precision=precision, preferred_element_type=F32
    )


def split(x):
    high = x.astype(BF16)
    rest = x - high.astype(F32)
    middle = rest.astype(BF16)
    return high, middle, (rest - middle.astype(F32)).astype(BF16)


def product(a, b):
    a_high, a_middle, a_low = split(a)
    b_high, b_middle, b_low = split(b)
    pair = jnp.concatenate([b_high, b_middle], axis=1)
    large = dot(
        jnp.concatenate([a_high, a_middle], axis=1), jnp.concatenate([pair, pair], axis=0)
    )
    small = dot(
        jnp.concatenate([a_low, a_high], axis=1), jnp.concatenate([b_high, b_low], axis=0)
    )
    columns = b.shape[1]
    return large[:, :columns] + (large[:, columns:] + small)


def divide(x, n):
    if n & (n - 1) == 0:
        return lax.shift_right_logical(x, jnp.full(x.shape, n.bit_length() - 1, x.dtype))
    return x // n


def rows_per_step(total, most):
    step = most
    while total % step:
        step //= 2
    return step


def gram_kernel(
    n_obs, n_cell,
    heads_in, well_in, count_in, obs_in, std_in, loc_in, taper_in, log_k_ref,
    gram_ref, cov_ref,
    heads_ref, well_ref, count_ref, std_ref, loc_ref, taper_ref, in_sem, field, squares,
    send_heads, mid_heads, recv_heads, send_idx, mid_idx, recv_idx,
    obs_send, obs_all, pred_send, pred_all, s_all, d_all, part, bands, band_sum, summed, field_sem, send_sem, recv_sem,
):
    total = n_obs * n_cell
    o, c = lax.axis_index("obs"), lax.axis_index("cell")
    cells, members = field.shape
    wells = obs_in.shape[0]
    slots = heads_ref.shape[0]
    piece_rows = cells // PIECES

    def piece_copy(p):
        rows = pl.ds(p * piece_rows, piece_rows)
        return pltpu.make_async_copy(log_k_ref.at[rows], field.at[rows], field_sem.at[p])

    inputs = [
        pltpu.make_async_copy(src, dst, in_sem.at[i])
        for i, (src, dst) in enumerate((
            (well_in, well_ref), (count_in, count_ref), (heads_in, heads_ref),
            (std_in, std_ref), (loc_in, loc_ref), (taper_in, taper_ref),
            (obs_in, obs_send.at[pl.ds(0, wells)]),
        ))
    ]
    for copy in inputs:
        copy.start()
    for p in range(PIECES):
        piece_copy(p).start()

    barrier = pltpu.get_barrier_semaphore()

    @pl.loop(1, n_obs)
    def _(i):
        pl.semaphore_signal(
            barrier, inc=1, device_id=(lax.rem(o + i, n_obs), c), device_id_type=MESH
        )

    @pl.loop(1, n_cell)
    def _(i):
        pl.semaphore_signal(
            barrier, inc=1, device_id=(o, lax.rem(c + i, n_cell)), device_id_type=MESH
        )

    for copy in inputs:
        copy.wait()

    well = well_ref[...]
    lane = lax.broadcasted_iota(jnp.int32, (1, slots), 1)
    owner = divide(well, wells)
    place_in = (well - owner * wells + 1).astype(F32)
    owner = jnp.where(lane < count_ref[0], owner, total)
    lane_f = lane.astype(F32)
    group = 8
    rows_now = group * CAP
    row_at = lax.broadcasted_iota(jnp.int32, (rows_now, 1), 0)
    in_group = divide(row_at, CAP)
    rank = (row_at - in_group * CAP).astype(F32)
    well_lane = lax.broadcasted_iota(jnp.int32, (1, wells), 1).astype(F32)

    @pl.loop(0, total // group)
    def _(i):
        dest = in_group + i * group
        start = jnp.sum(jnp.where(owner < dest, 1.0, 0.0), axis=1, keepdims=True)
        hit = jnp.where((owner == dest) & (lane_f == start + rank), 1.0, 0.0)
        rows = pl.ds(pl.multiple_of(i * rows_now, rows_now), rows_now)
        send_heads[rows, :] = dot(hit.astype(BF16), heads_ref[...]).astype(BF16)
        place = jnp.sum(hit * place_in, axis=1, keepdims=True) - 1.0
        ranks = jnp.where(place == well_lane, rank + 1.0, 0.0)
        for q in range(group):
            send_idx[i * group + q] = (
                jnp.sum(ranks[q * CAP : (q + 1) * CAP], axis=0, keepdims=True) - 1.0
            )

    obs_send[wells:, :] = jnp.broadcast_to(std_ref[...], (8, wells))
    pl.semaphore_wait(barrier, n_obs + n_cell - 2)

    def to_obs(src_of, dst, at):
        @pl.loop(1, n_obs)
        def _(i):
            to = lax.rem(o + i, n_obs)
            pltpu.make_async_remote_copy(
                src_ref=src_of(to), dst_ref=dst.at[o], send_sem=send_sem.at[at],
                recv_sem=recv_sem.at[at], device_id=(to, c), device_id_type=MESH,
            ).start()

        pltpu.make_async_copy(src_of(o), dst.at[o], recv_sem.at[at]).start()

    def to_cells(src_of, dst, at):
        @pl.loop(1, n_cell)
        def _(i):
            to = lax.rem(c + i, n_cell)
            pltpu.make_async_remote_copy(
                src_ref=src_of(to), dst_ref=dst.at[c], send_sem=send_sem.at[at],
                recv_sem=recv_sem.at[at], device_id=(o, to), device_id_type=MESH,
            ).start()

        pltpu.make_async_copy(src_of(c), dst.at[c], recv_sem.at[at]).start()

    line = n_cell * CAP
    to_obs(lambda to: send_heads.at[pl.ds(pl.multiple_of(to * line, line), line)], mid_heads, 0)
    to_obs(lambda to: send_idx.at[pl.ds(to * n_cell, n_cell)], mid_idx, 1)
    to_cells(lambda to: obs_send, obs_all, 2)

    square = (members, members)
    centring = jnp.where(
        lax.broadcasted_iota(jnp.int32, square, 0) == lax.broadcasted_iota(jnp.int32, square, 1),
        1.0 - 1.0 / members, -1.0 / members,
    ).astype(BF16)
    step_rows = rows_per_step(piece_rows, 1024)
    squares[...] = jnp.zeros_like(squares)

    def covariance(p):
        piece_copy(p).wait()

        @pl.loop(0, piece_rows // step_rows)
        def _(i):
            at = pl.multiple_of(p * piece_rows + i * step_rows, step_rows)
            x = field[pl.ds(at, step_rows), :]
            anomalies = lax.dot_general(
                centring, x, (((1,), (1,)), ((), ())), preferred_element_type=F32
            )
            squares[...] += dot(anomalies.astype(BF16), x)

    def arrived(ref, at):
        pltpu.make_async_copy(ref, ref, recv_sem.at[at]).wait()

    covariance(0)
    arrived(mid_heads, 0)
    arrived(mid_idx, 1)
    to_cells(lambda to: mid_heads.at[:, pl.ds(pl.multiple_of(to * CAP, CAP), CAP)], recv_heads, 6)
    to_cells(lambda to: mid_idx.at[:, to], recv_idx, 7)
    covariance(1)
    arrived(recv_heads, 6)
    arrived(recv_idx, 7)
    ranks_at = lax.broadcasted_iota(jnp.int32, (total, CAP, wells), 1).astype(F32)
    ranks = recv_idx[...].reshape(total, 1, wells)
    take = jnp.where(ranks == ranks_at, 1.0, 0.0).reshape(total * CAP, wells)
    heads = recv_heads[...].reshape(total * CAP, members)
    pred_send[...] = dot_rows(take.astype(BF16), heads).astype(BF16)
    to_cells(lambda to: pred_send, pred_all, 3)

    covariance(2)
    covariance(3)
    arrived(obs_all, 2)
    arrived(pred_all, 3)
    eye = (
        lax.broadcasted_iota(jnp.int32, (wells, wells), 0)
        == lax.broadcasted_iota(jnp.int32, (wells, wells), 1)
    )

    @pl.loop(0, n_cell)
    def _(b):
        block = o * n_cell + b
        weight = jnp.sum(
            jnp.where(loc_ref[pl.ds(c, 1), :] == block, taper_ref[pl.ds(c, 1), :], 0.0),
            axis=1, keepdims=True,
        )
        std = jnp.sum(
            jnp.where(eye, obs_all[b, pl.ds(wells, 1), :], 0.0), axis=1, keepdims=True
        )
        inverse = 1.0 / std
        pred = pred_all[b].astype(F32)
        mean = jnp.mean(pred, axis=1, keepdims=True)
        scaled = (pred - mean) * inverse
        rows = pl.ds(pl.multiple_of(b * wells, wells), wells)
        s_all[rows, :] = scaled * weight
        d_all[rows, :members] = scaled
        d_all[rows, members:] = (obs_all[b, pl.ds(0, wells), :] - pred) * inverse

    product = dot_rows(s_all[...], d_all[...], HIGHEST)
    band = members // n_obs
    part[...] = product.reshape(part.shape)

    to_obs(lambda to: part.at[to], bands, 4)
    covariance(4)
    arrived(bands, 4)
    band_sum[...] = jnp.sum(bands[...], axis=0)
    to_obs(lambda to: band_sum, summed, 5)
    covariance(5)
    arrived(summed, 5)
    gram_ref[...] = summed[...].reshape(gram_ref.shape)
    cov_ref[...] = squares[...] - jnp.mean(squares[...], axis=1, keepdims=True)

    def sent(ref, at):
        pltpu.make_async_copy(ref, ref, send_sem.at[at]).wait()

    sent(mid_heads.at[pl.ds(0, n_obs - 1)], 0)
    sent(mid_idx.at[pl.ds(0, n_obs - 1)], 1)
    sent(recv_heads.at[pl.ds(0, n_cell - 1)], 6)
    sent(recv_idx.at[pl.ds(0, n_cell - 1)], 7)
    sent(obs_all.at[pl.ds(0, n_cell - 1)], 2)
    sent(pred_all.at[pl.ds(0, n_cell - 1)], 3)
    sent(bands.at[pl.ds(0, n_obs - 1)], 4)
    sent(summed.at[pl.ds(0, n_obs - 1)], 5)


def update_kernel(
    gram_ref, cov_ref, lambda_ref, log_k_ref, posterior_ref, norms_ref,
    field, inverse, weights, in_sem, out_sem,
):
    cells, members = field.shape
    groups = in_sem.shape[0]
    group_rows = cells // groups
    lambda_total = lambda_ref.shape[0]

    def group_copy(g, back):
        rows = pl.ds(g * group_rows, group_rows)
        if back:
            return pltpu.make_async_copy(field.at[rows], posterior_ref.at[rows], out_sem.at[g])
        return pltpu.make_async_copy(log_k_ref.at[rows], field.at[rows], in_sem.at[g])

    for g in range(groups):
        group_copy(g, False).start()

    curvature = gram_ref[:, :members]
    square = product(curvature, curvature)
    top = jnp.sqrt(jnp.max(jnp.sum(jnp.abs(square), axis=1, keepdims=True)))
    top = jnp.minimum(top, jnp.max(jnp.sum(jnp.abs(curvature), axis=1, keepdims=True)))
    cube = product(square, curvature)
    eye = jnp.where(
        lax.broadcasted_iota(jnp.int32, (members, members), 0)
        == lax.broadcasted_iota(jnp.int32, (members, members), 1),
        1.0, 0.0,
    )
    shifts = [(1.0 + lambda_ref[l]) * (members - 1) for l in range(lambda_total)]

    def advance(rho):
        return 2.0 / (2.0 - rho * rho), rho * rho / (2.0 - rho * rho)

    def block(l):
        return pl.ds(l * members, members)

    rhos = []
    for l in range(lambda_total):
        shift = shifts[l]
        first = 2.0 / (2.0 * shift + top)
        gain, rho = advance(top * (0.5 * first))
        u, v = 2.0 * gain * first, gain * first * first
        gain, rho = advance(rho)
        terms = (
            2.0 * u - 2.0 * v * shift - shift * (u - v * shift) * (u - v * shift),
            -2.0 * v - (u - v * shift) * (u - 3.0 * v * shift),
            v * (2.0 * u - 3.0 * v * shift),
            -v * v,
        )
        inverse[block(l), :] = gain * (
            terms[0] * eye + terms[1] * curvature + terms[2] * square + terms[3] * cube
        )
        rhos.append(rho)

    def largest(values):
        return functools.reduce(jnp.maximum, values)

    def step(carry):
        count, rhos = carry
        after = []
        shared = product(inverse[...], gram_ref[:, :members])
        for l in range(lambda_total):
            gain, rho = advance(rhos[l])
            x = inverse[block(l), :]
            half = shared[l * members : (l + 1) * members] + shifts[l] * x
            inverse[block(l), :] = gain * (2.0 * x - product(half, x))
            after.append(rho)
        return count + 1, tuple(after)

    lax.while_loop(
        lambda carry: (largest(carry[1]) > 3e-5) & (carry[0] < 40),
        step,
        (jnp.int32(0), tuple(rhos)),
    )

    solved = product(inverse[...], gram_ref[:, members:]).astype(BF16)
    transform = solved[:members].astype(F32)
    centred = transform - jnp.mean(transform, axis=0, keepdims=True) + eye
    high = centred.astype(BF16)
    weights[:members, :] = high
    weights[members:, :] = (centred - high.astype(F32)).astype(BF16)

    step_rows = rows_per_step(group_rows, 2048)
    half_rows = step_rows // 2
    for g in range(groups):
        group_copy(g, False).wait()

        @pl.loop(0, group_rows // step_rows)
        def _(i):
            at = pl.multiple_of(g * group_rows + i * step_rows, step_rows)
            upper, lower = pl.ds(at, half_rows), pl.ds(at + half_rows, half_rows)
            for rows in (upper, lower):
                x = field[rows, :]
                field[rows, :] = dot(jnp.concatenate([x, x], axis=1), weights[...]).astype(BF16)

        group_copy(g, True).start()

    beside = jnp.concatenate(
        [solved[l * members : (l + 1) * members] for l in range(lambda_total)], axis=1
    )
    high, middle, low = split(cov_ref[...])
    spread = dot(
        jnp.concatenate([high, middle], axis=1), jnp.concatenate([beside, beside], axis=0)
    ) + dot(low, beside)
    norms = jnp.sum(beside.astype(F32) * spread, axis=0, keepdims=True)
    for l in range(lambda_total):
        norms_ref[pl.ds(l, 1), :] = norms[:, l * members : (l + 1) * members]
    for g in range(groups):
        group_copy(g, True).wait()


def on_device(
    log_k, heads_pred, slot_well, tile_count, obs_values, obs_std, loc_blocks, taper, lambdas
):
    n_obs = lax.axis_size("obs")
    n_cell = lax.axis_size("cell")
    total = n_obs * n_cell
    cells, members = log_k.shape
    slots = slot_well.shape[0]
    wells = obs_values.shape[0]
    band = members // n_obs
    vmem = pl.BlockSpec(memory_space=pltpu.VMEM)
    smem = pl.BlockSpec(memory_space=pltpu.SMEM)
    hbm = pl.BlockSpec(memory_space=pl.ANY)
    gram, cov = pl.pallas_call(
        functools.partial(gram_kernel, n_obs, n_cell),
        out_shape=(
            jax.ShapeDtypeStruct((members, 2 * members), F32),
            jax.ShapeDtypeStruct((members, members), F32),
        ),
        in_specs=[hbm] * 8,
        out_specs=(vmem, vmem),
        scratch_shapes=[
            pltpu.VMEM((slots, members), BF16),
            pltpu.VMEM((1, slots), jnp.int32),
            pltpu.SMEM((1,), jnp.int32),
            pltpu.VMEM((1, wells), F32),
            pltpu.VMEM(loc_blocks.shape, jnp.int32),
            pltpu.VMEM(taper.shape, F32),
            pltpu.SemaphoreType.DMA((7,)),
            pltpu.VMEM((cells, members), BF16),
            pltpu.VMEM((members, members), F32),
            pltpu.VMEM((total * CAP, members), BF16),
            pltpu.VMEM((n_obs, n_cell * CAP, members), BF16),
            pltpu.VMEM((n_cell, n_obs, CAP, members), BF16),
            pltpu.VMEM((total, 1, wells), F32),
            pltpu.VMEM((n_obs, n_cell, 1, wells), F32),
            pltpu.VMEM((n_cell, n_obs, 1, wells), F32),
            pltpu.VMEM((wells + 8, members), F32),
            pltpu.VMEM((n_cell, wells + 8, members), F32),
            pltpu.VMEM((wells, members), BF16),
            pltpu.VMEM((n_cell, wells, members), BF16),
            pltpu.VMEM((n_cell * wells, members), F32),
            pltpu.VMEM((n_cell * wells, 2 * members), F32),
            pltpu.VMEM((n_obs, band, 2 * members), F32),
            pltpu.VMEM((n_obs, band, 2 * members), F32),
            pltpu.VMEM((band, 2 * members), F32),
            pltpu.VMEM((n_obs, band, 2 * members), F32),
            pltpu.SemaphoreType.DMA((PIECES,)),
            pltpu.SemaphoreType.DMA((8,)),
            pltpu.SemaphoreType.DMA((8,)),
        ],
        compiler_params=pltpu.CompilerParams(
            collective_id=0, has_side_effects=True, vmem_limit_bytes=60 << 20
        ),
        name="gram",
    )(
        heads_pred, slot_well.reshape(1, slots), tile_count, obs_values,
        obs_std.reshape(1, wells), loc_blocks, taper, log_k,
    )
    lambda_total = lambdas.shape[0]
    groups = 12
    posterior, norms = pl.pallas_call(
        update_kernel,
        out_shape=(
            jax.ShapeDtypeStruct((cells, members), BF16),
            jax.ShapeDtypeStruct((lambda_total, members), F32),
        ),
        in_specs=[vmem, vmem, smem, hbm],
        out_specs=(hbm, vmem),
        scratch_shapes=[
            pltpu.VMEM((cells, members), BF16),
            pltpu.VMEM((lambda_total * members, members), F32),
            pltpu.VMEM((2 * members, members), BF16),
            pltpu.SemaphoreType.DMA((groups,)),
            pltpu.SemaphoreType.DMA((groups,)),
        ],
        compiler_params=pltpu.CompilerParams(vmem_limit_bytes=60 << 20),
        name="update",
    )(gram, cov, lambdas, log_k)
    return posterior, norms[None]


def solution(mesh):
    return jax.shard_map(
        on_device,
        mesh=mesh,
        in_specs=(
            P(("obs", "cell"), None),
            P(("obs", "cell"), None),
            P(("obs", "cell")),
            P(("obs", "cell")),
            P(("obs", "cell"), None),
            P(("obs", "cell")),
            P(),
            P(),
            P(),
        ),
        out_specs=(P(("obs", "cell"), None), P(("obs", "cell"), None, None)),
        check_vma=False,
    )
```

```python
import functools

import jax
import jax.numpy as jnp
from jax import lax
from jax.experimental import pallas as pl
from jax.experimental.pallas import tpu as pltpu
from jax.sharding import PartitionSpec as P

CAP = 16
PIECES = 6
MESH = pl.DeviceIdType.MESH
HIGHEST = lax.Precision.HIGHEST
F32 = jnp.float32
BF16 = jnp.bfloat16


def dot(a, b, precision=None):
    return jnp.dot(a, b, precision=precision, preferred_element_type=F32)


def dot_rows(a, b, precision=None):
    return lax.dot_general(
        a, b, (((0,), (0,)), ((), ())), precision=precision, preferred_element_type=F32
    )


def split(x):
    high = x.astype(BF16)
    rest = x - high.astype(F32)
    middle = rest.astype(BF16)
    return high, middle, (rest - middle.astype(F32)).astype(BF16)


def product(a, b):
    a_high, a_middle, a_low = split(a)
    b_high, b_middle, b_low = split(b)
    pair = jnp.concatenate([b_high, b_middle], axis=1)
    large = dot(
        jnp.concatenate([a_high, a_middle], axis=1), jnp.concatenate([pair, pair], axis=0)
    )
    small = dot(
        jnp.concatenate([a_low, a_high], axis=1), jnp.concatenate([b_high, b_low], axis=0)
    )
    columns = b.shape[1]
    return large[:, :columns] + (large[:, columns:] + small)


def divide(x, n):
    if n & (n - 1) == 0:
        return lax.shift_right_logical(x, jnp.full(x.shape, n.bit_length() - 1, x.dtype))
    return x // n


def rows_per_step(total, most):
    step = most
    while total % step:
        step //= 2
    return step


def gram_kernel(
    n_obs, n_cell,
    heads_in, well_in, count_in, obs_in, std_in, loc_in, taper_in, log_k_ref,
    gram_ref, cov_ref,
    heads_ref, well_ref, count_ref, std_ref, loc_ref, taper_ref, in_sem, field, squares,
    send_heads, mid_heads, recv_heads, send_idx, mid_idx, recv_idx,
    obs_ref, part, terms, got, bands, band_sum, summed, field_sem, send_sem, recv_sem,
):
    total = n_obs * n_cell
    o, c = lax.axis_index("obs"), lax.axis_index("cell")
    cells, members = field.shape
    wells = obs_in.shape[0]
    slots = heads_ref.shape[0]
    piece_rows = cells // PIECES

    def piece_copy(p):
        rows = pl.ds(p * piece_rows, piece_rows)
        return pltpu.make_async_copy(log_k_ref.at[rows], field.at[rows], field_sem.at[p])

    inputs = [
        pltpu.make_async_copy(src, dst, in_sem.at[i])
        for i, (src, dst) in enumerate((
            (well_in, well_ref), (count_in, count_ref), (heads_in, heads_ref),
            (std_in, std_ref), (loc_in, loc_ref), (taper_in, taper_ref),
            (obs_in, obs_ref),
        ))
    ]
    for copy in inputs:
        copy.start()
    for p in range(PIECES):
        piece_copy(p).start()

    barrier = pltpu.get_barrier_semaphore()

    @pl.loop(1, n_obs)
    def _(i):
        pl.semaphore_signal(
            barrier, inc=1, device_id=(lax.rem(o + i, n_obs), c), device_id_type=MESH
        )

    @pl.loop(1, n_cell)
    def _(i):
        pl.semaphore_signal(
            barrier, inc=1, device_id=(o, lax.rem(c + i, n_cell)), device_id_type=MESH
        )

    for copy in inputs:
        copy.wait()

    well = well_ref[...]
    lane = lax.broadcasted_iota(jnp.int32, (1, slots), 1)
    owner = divide(well, wells)
    place_in = (well - owner * wells + 1).astype(F32)
    owner = jnp.where(lane < count_ref[0], owner, total)
    lane_f = lane.astype(F32)
    group = 8
    rows_now = group * CAP
    row_at = lax.broadcasted_iota(jnp.int32, (rows_now, 1), 0)
    in_group = divide(row_at, CAP)
    rank = (row_at - in_group * CAP).astype(F32)
    well_lane = lax.broadcasted_iota(jnp.int32, (1, wells), 1).astype(F32)

    @pl.loop(0, total // group)
    def _(i):
        dest = in_group + i * group
        start = jnp.sum(jnp.where(owner < dest, 1.0, 0.0), axis=1, keepdims=True)
        hit = jnp.where((owner == dest) & (lane_f == start + rank), 1.0, 0.0)
        rows = pl.ds(pl.multiple_of(i * rows_now, rows_now), rows_now)
        send_heads[rows, :] = dot(hit.astype(BF16), heads_ref[...]).astype(BF16)
        place = jnp.sum(hit * place_in, axis=1, keepdims=True) - 1.0
        ranks = jnp.where(place == well_lane, rank + 1.0, 0.0)
        for q in range(group):
            send_idx[i * group + q] = (
                jnp.sum(ranks[q * CAP : (q + 1) * CAP], axis=0, keepdims=True) - 1.0
            )

    pl.semaphore_wait(barrier, n_obs + n_cell - 2)

    def to_obs(src_of, dst, at):
        @pl.loop(1, n_obs)
        def _(i):
            to = lax.rem(o + i, n_obs)
            pltpu.make_async_remote_copy(
                src_ref=src_of(to), dst_ref=dst.at[o], send_sem=send_sem.at[at],
                recv_sem=recv_sem.at[at], device_id=(to, c), device_id_type=MESH,
            ).start()

        pltpu.make_async_copy(src_of(o), dst.at[o], recv_sem.at[at]).start()

    def to_cells(src_of, dst, at):
        @pl.loop(1, n_cell)
        def _(i):
            to = lax.rem(c + i, n_cell)
            pltpu.make_async_remote_copy(
                src_ref=src_of(to), dst_ref=dst.at[c], send_sem=send_sem.at[at],
                recv_sem=recv_sem.at[at], device_id=(o, to), device_id_type=MESH,
            ).start()

        pltpu.make_async_copy(src_of(c), dst.at[c], recv_sem.at[at]).start()

    line = n_cell * CAP
    to_obs(lambda to: send_heads.at[pl.ds(pl.multiple_of(to * line, line), line)], mid_heads, 0)
    to_obs(lambda to: send_idx.at[pl.ds(to * n_cell, n_cell)], mid_idx, 1)

    square = (members, members)
    centring = jnp.where(
        lax.broadcasted_iota(jnp.int32, square, 0) == lax.broadcasted_iota(jnp.int32, square, 1),
        1.0 - 1.0 / members, -1.0 / members,
    ).astype(BF16)
    step_rows = rows_per_step(piece_rows, 1024)
    squares[...] = jnp.zeros_like(squares)

    def covariance(p):
        piece_copy(p).wait()

        @pl.loop(0, piece_rows // step_rows)
        def _(i):
            at = pl.multiple_of(p * piece_rows + i * step_rows, step_rows)
            x = field[pl.ds(at, step_rows), :]
            anomalies = lax.dot_general(
                centring, x, (((1,), (1,)), ((), ())), preferred_element_type=F32
            )
            squares[...] += dot(anomalies.astype(BF16), x)

    def arrived(ref, at):
        pltpu.make_async_copy(ref, ref, recv_sem.at[at]).wait()

    eye = (
        lax.broadcasted_iota(jnp.int32, (wells, wells), 0)
        == lax.broadcasted_iota(jnp.int32, (wells, wells), 1)
    )
    inverse = 1.0 / jnp.sum(jnp.where(eye, std_ref[...], 0.0), axis=1, keepdims=True)
    tile_weights = [
        jnp.sum(
            jnp.where(loc_ref[...] == b * n_cell + c, taper_ref[...], 0.0),
            axis=1, keepdims=True,
        )
        for b in range(n_obs)
    ]

    covariance(0)
    arrived(mid_heads, 0)
    arrived(mid_idx, 1)
    to_cells(lambda to: mid_heads.at[:, pl.ds(pl.multiple_of(to * CAP, CAP), CAP)], recv_heads, 2)
    to_cells(lambda to: mid_idx.at[:, to], recv_idx, 6)
    covariance(1)
    arrived(recv_heads, 2)
    arrived(recv_idx, 6)
    ranks_at = lax.broadcasted_iota(jnp.int32, (total, CAP, wells), 1).astype(F32)
    ranks = recv_idx[...].reshape(total, 1, wells)
    take = jnp.where(ranks == ranks_at, 1.0, 0.0).reshape(total * CAP, wells)
    heads = recv_heads[...].reshape(total * CAP, members)
    pred = dot_rows(take.astype(BF16), heads)
    scaled = (pred - jnp.mean(pred, axis=1, keepdims=True)) * inverse
    innovation = (obs_ref[...] - pred) * inverse
    joined = jnp.concatenate([scaled, innovation], axis=1)
    part[...] = dot_rows(scaled, joined, HIGHEST).reshape(part.shape)
    to_obs(lambda to: part.at[to], bands, 4)
    covariance(2)
    arrived(bands, 4)
    for t in range(n_cell):
        terms[t] = sum(tile_weights[b][t : t + 1, :] * bands[b] for b in range(n_obs))
    to_cells(lambda to: terms.at[to], got, 3)
    covariance(3)
    covariance(4)
    arrived(got, 3)
    band_sum[...] = jnp.sum(got[...], axis=0)
    to_obs(lambda to: band_sum, summed, 5)
    covariance(5)
    arrived(summed, 5)
    gram_ref[...] = summed[...].reshape(gram_ref.shape)
    cov_ref[...] = squares[...] - jnp.mean(squares[...], axis=1, keepdims=True)

    def sent(ref, at):
        pltpu.make_async_copy(ref, ref, send_sem.at[at]).wait()

    sent(mid_heads.at[pl.ds(0, n_obs - 1)], 0)
    sent(mid_idx.at[pl.ds(0, n_obs - 1)], 1)
    sent(recv_heads.at[pl.ds(0, n_cell - 1)], 2)
    sent(recv_idx.at[pl.ds(0, n_cell - 1)], 6)
    sent(got.at[pl.ds(0, n_cell - 1)], 3)
    sent(bands.at[pl.ds(0, n_obs - 1)], 4)
    sent(summed.at[pl.ds(0, n_obs - 1)], 5)


def update_kernel(
    gram_ref, cov_ref, lambda_ref, log_k_ref, posterior_ref, norms_ref,
    field, inverse, weights, in_sem, out_sem,
):
    cells, members = field.shape
    groups = in_sem.shape[0]
    group_rows = cells // groups
    lambda_total = lambda_ref.shape[0]

    def group_copy(g, back):
        rows = pl.ds(g * group_rows, group_rows)
        if back:
            return pltpu.make_async_copy(field.at[rows], posterior_ref.at[rows], out_sem.at[g])
        return pltpu.make_async_copy(log_k_ref.at[rows], field.at[rows], in_sem.at[g])

    for g in range(groups):
        group_copy(g, False).start()

    curvature = gram_ref[:, :members]
    square = product(curvature, curvature)
    top = jnp.sqrt(jnp.max(jnp.sum(jnp.abs(square), axis=1, keepdims=True)))
    top = jnp.minimum(top, jnp.max(jnp.sum(jnp.abs(curvature), axis=1, keepdims=True)))
    cube = product(square, curvature)
    eye = jnp.where(
        lax.broadcasted_iota(jnp.int32, (members, members), 0)
        == lax.broadcasted_iota(jnp.int32, (members, members), 1),
        1.0, 0.0,
    )
    shifts = [(1.0 + lambda_ref[l]) * (members - 1) for l in range(lambda_total)]

    def advance(rho):
        return 2.0 / (2.0 - rho * rho), rho * rho / (2.0 - rho * rho)

    def block(l):
        return pl.ds(l * members, members)

    rhos = []
    for l in range(lambda_total):
        shift = shifts[l]
        first = 2.0 / (2.0 * shift + top)
        gain, rho = advance(top * (0.5 * first))
        u, v = 2.0 * gain * first, gain * first * first
        gain, rho = advance(rho)
        terms = (
            2.0 * u - 2.0 * v * shift - shift * (u - v * shift) * (u - v * shift),
            -2.0 * v - (u - v * shift) * (u - 3.0 * v * shift),
            v * (2.0 * u - 3.0 * v * shift),
            -v * v,
        )
        inverse[block(l), :] = gain * (
            terms[0] * eye + terms[1] * curvature + terms[2] * square + terms[3] * cube
        )
        rhos.append(rho)

    def largest(values):
        return functools.reduce(jnp.maximum, values)

    def step(carry):
        count, rhos = carry
        after = []
        shared = product(inverse[...], gram_ref[:, :members])
        for l in range(lambda_total):
            gain, rho = advance(rhos[l])
            x = inverse[block(l), :]
            half = shared[l * members : (l + 1) * members] + shifts[l] * x
            inverse[block(l), :] = gain * (2.0 * x - product(half, x))
            after.append(rho)
        return count + 1, tuple(after)

    lax.while_loop(
        lambda carry: (largest(carry[1]) > 3e-5) & (carry[0] < 40),
        step,
        (jnp.int32(0), tuple(rhos)),
    )

    solved = product(inverse[...], gram_ref[:, members:]).astype(BF16)
    transform = solved[:members].astype(F32)
    centred = transform - jnp.mean(transform, axis=0, keepdims=True) + eye
    high = centred.astype(BF16)
    low = (centred - high.astype(F32)).astype(BF16)
    none = jnp.zeros_like(high)
    weights[:members, :] = jnp.concatenate([high, none, low, none], axis=1)
    weights[members:, :] = jnp.concatenate([none, high, none, low], axis=1)

    step_rows = rows_per_step(group_rows, 1024)
    half_rows = step_rows // 2
    for g in range(groups):
        group_copy(g, False).wait()

        @pl.loop(0, group_rows // step_rows)
        def _(i):
            at = pl.multiple_of(g * group_rows + i * step_rows, step_rows)
            upper, lower = pl.ds(at, half_rows), pl.ds(at + half_rows, half_rows)
            x = jnp.concatenate([field[upper, :], field[lower, :]], axis=1)
            both = dot(x, weights[...])
            both = (both[:, : 2 * members] + both[:, 2 * members :]).astype(BF16)
            field[upper, :] = both[:, :members]
            field[lower, :] = both[:, members:]

        group_copy(g, True).start()

    beside = jnp.concatenate(
        [solved[l * members : (l + 1) * members] for l in range(lambda_total)], axis=1
    )
    high, middle, low = split(cov_ref[...])
    spread = dot(
        jnp.concatenate([high, middle], axis=1), jnp.concatenate([beside, beside], axis=0)
    ) + dot(low, beside)
    norms = jnp.sum(beside.astype(F32) * spread, axis=0, keepdims=True)
    for l in range(lambda_total):
        norms_ref[pl.ds(l, 1), :] = norms[:, l * members : (l + 1) * members]
    for g in range(groups):
        group_copy(g, True).wait()


def on_device(
    log_k, heads_pred, slot_well, tile_count, obs_values, obs_std, loc_blocks, taper, lambdas
):
    n_obs = lax.axis_size("obs")
    n_cell = lax.axis_size("cell")
    total = n_obs * n_cell
    cells, members = log_k.shape
    slots = slot_well.shape[0]
    wells = obs_values.shape[0]
    band = members // n_obs
    vmem = pl.BlockSpec(memory_space=pltpu.VMEM)
    smem = pl.BlockSpec(memory_space=pltpu.SMEM)
    hbm = pl.BlockSpec(memory_space=pl.ANY)
    gram, cov = pl.pallas_call(
        functools.partial(gram_kernel, n_obs, n_cell),
        out_shape=(
            jax.ShapeDtypeStruct((members, 2 * members), F32),
            jax.ShapeDtypeStruct((members, members), F32),
        ),
        in_specs=[hbm] * 8,
        out_specs=(vmem, vmem),
        scratch_shapes=[
            pltpu.VMEM((slots, members), BF16),
            pltpu.VMEM((1, slots), jnp.int32),
            pltpu.SMEM((1,), jnp.int32),
            pltpu.VMEM((1, wells), F32),
            pltpu.VMEM(loc_blocks.shape, jnp.int32),
            pltpu.VMEM(taper.shape, F32),
            pltpu.SemaphoreType.DMA((7,)),
            pltpu.VMEM((cells, members), BF16),
            pltpu.VMEM((members, members), F32),
            pltpu.VMEM((total * CAP, members), BF16),
            pltpu.VMEM((n_obs, n_cell * CAP, members), BF16),
            pltpu.VMEM((n_cell, n_obs, CAP, members), BF16),
            pltpu.VMEM((total, 1, wells), F32),
            pltpu.VMEM((n_obs, n_cell, 1, wells), F32),
            pltpu.VMEM((n_cell, n_obs, 1, wells), F32),
            pltpu.VMEM((wells, members), F32),
            pltpu.VMEM((n_obs, band, 2 * members), F32),
            pltpu.VMEM((n_cell, band, 2 * members), F32),
            pltpu.VMEM((n_cell, band, 2 * members), F32),
            pltpu.VMEM((n_obs, band, 2 * members), F32),
            pltpu.VMEM((band, 2 * members), F32),
            pltpu.VMEM((n_obs, band, 2 * members), F32),
            pltpu.SemaphoreType.DMA((PIECES,)),
            pltpu.SemaphoreType.DMA((7,)),
            pltpu.SemaphoreType.DMA((7,)),
        ],
        compiler_params=pltpu.CompilerParams(
            collective_id=0, has_side_effects=True, vmem_limit_bytes=60 << 20
        ),
        name="gram",
    )(
        heads_pred, slot_well.reshape(1, slots), tile_count, obs_values,
        obs_std.reshape(1, wells), loc_blocks, taper, log_k,
    )
    lambda_total = lambdas.shape[0]
    groups = 12
    posterior, norms = pl.pallas_call(
        update_kernel,
        out_shape=(
            jax.ShapeDtypeStruct((cells, members), BF16),
            jax.ShapeDtypeStruct((lambda_total, members), F32),
        ),
        in_specs=[vmem, vmem, smem, hbm],
        out_specs=(hbm, vmem),
        scratch_shapes=[
            pltpu.VMEM((cells, members), BF16),
            pltpu.VMEM((lambda_total * members, members), F32),
            pltpu.VMEM((2 * members, 4 * members), BF16),
            pltpu.SemaphoreType.DMA((groups,)),
            pltpu.SemaphoreType.DMA((groups,)),
        ],
        compiler_params=pltpu.CompilerParams(vmem_limit_bytes=60 << 20),
        name="update",
    )(gram, cov, lambdas, log_k)
    return posterior, norms[None]


def solution(mesh):
    return jax.shard_map(
        on_device,
        mesh=mesh,
        in_specs=(
            P(("obs", "cell"), None),
            P(("obs", "cell"), None),
            P(("obs", "cell")),
            P(("obs", "cell")),
            P(("obs", "cell"), None),
            P(("obs", "cell")),
            P(),
            P(),
            P(),
        ),
        out_specs=(P(("obs", "cell"), None), P(("obs", "cell"), None, None)),
        check_vma=False,
    )
```

```python
import functools

import jax
import jax.numpy as jnp
from jax import lax
from jax.experimental import pallas as pl
from jax.experimental.pallas import tpu as pltpu
from jax.sharding import PartitionSpec as P

CAP = 16
PIECES = 6
MESH = pl.DeviceIdType.MESH
HIGHEST = lax.Precision.HIGHEST
F32 = jnp.float32
BF16 = jnp.bfloat16


def dot(a, b, precision=None):
    return jnp.dot(a, b, precision=precision, preferred_element_type=F32)


def dot_rows(a, b, precision=None):
    return lax.dot_general(
        a, b, (((0,), (0,)), ((), ())), precision=precision, preferred_element_type=F32
    )


def split(x):
    high = x.astype(BF16)
    rest = x - high.astype(F32)
    middle = rest.astype(BF16)
    return high, middle, (rest - middle.astype(F32)).astype(BF16)


def product(a, b):
    a_high, a_middle, a_low = split(a)
    b_high, b_middle, b_low = split(b)
    pair = jnp.concatenate([b_high, b_middle], axis=1)
    large = dot(
        jnp.concatenate([a_high, a_middle], axis=1), jnp.concatenate([pair, pair], axis=0)
    )
    small = dot(
        jnp.concatenate([a_low, a_high], axis=1), jnp.concatenate([b_high, b_low], axis=0)
    )
    columns = b.shape[1]
    return large[:, :columns] + (large[:, columns:] + small)


def divide(x, n):
    if n & (n - 1) == 0:
        return lax.shift_right_logical(x, jnp.full(x.shape, n.bit_length() - 1, x.dtype))
    return x // n


def rows_per_step(total, most):
    step = most
    while total % step:
        step //= 2
    return step


def gram_kernel(
    n_obs, n_cell,
    heads_in, well_in, count_in, obs_in, std_in, loc_in, taper_in, log_k_ref,
    gram_ref, cov_ref,
    heads_ref, well_ref, count_ref, std_ref, loc_ref, taper_ref, in_sem, field, squares,
    send_heads, mid_heads, recv_heads, send_idx, mid_idx, recv_idx,
    obs_ref, part, terms, got, bands, band_sum, summed, field_sem, send_sem, recv_sem,
):
    total = n_obs * n_cell
    o, c = lax.axis_index("obs"), lax.axis_index("cell")
    cells, members = field.shape
    wells = obs_in.shape[0]
    slots = heads_ref.shape[0]
    piece_rows = cells // PIECES

    def piece_copy(p):
        rows = pl.ds(p * piece_rows, piece_rows)
        return pltpu.make_async_copy(log_k_ref.at[rows], field.at[rows], field_sem.at[p])

    inputs = [
        pltpu.make_async_copy(src, dst, in_sem.at[i])
        for i, (src, dst) in enumerate((
            (well_in, well_ref), (count_in, count_ref), (heads_in, heads_ref),
            (std_in, std_ref), (loc_in, loc_ref), (taper_in, taper_ref),
            (obs_in, obs_ref),
        ))
    ]
    for copy in inputs:
        copy.start()
    for p in range(PIECES):
        piece_copy(p).start()

    barrier = pltpu.get_barrier_semaphore()

    @pl.loop(1, n_obs)
    def _(i):
        pl.semaphore_signal(
            barrier, inc=1, device_id=(lax.rem(o + i, n_obs), c), device_id_type=MESH
        )

    @pl.loop(1, n_cell)
    def _(i):
        pl.semaphore_signal(
            barrier, inc=1, device_id=(o, lax.rem(c + i, n_cell)), device_id_type=MESH
        )

    for copy in inputs:
        copy.wait()

    well = well_ref[...]
    lane = lax.broadcasted_iota(jnp.int32, (1, slots), 1)
    owner = divide(well, wells)
    place_in = (well - owner * wells + 1).astype(F32)
    owner = jnp.where(lane < count_ref[0], owner, total)
    lane_f = lane.astype(F32)
    group = 8
    rows_now = group * CAP
    row_at = lax.broadcasted_iota(jnp.int32, (rows_now, 1), 0)
    in_group = divide(row_at, CAP)
    rank = (row_at - in_group * CAP).astype(F32)
    well_lane = lax.broadcasted_iota(jnp.int32, (1, wells), 1).astype(F32)

    @pl.loop(0, total // group)
    def _(i):
        dest = in_group + i * group
        start = jnp.sum(jnp.where(owner < dest, 1.0, 0.0), axis=1, keepdims=True)
        hit = jnp.where((owner == dest) & (lane_f == start + rank), 1.0, 0.0)
        rows = pl.ds(pl.multiple_of(i * rows_now, rows_now), rows_now)
        send_heads[rows, :] = dot(hit.astype(BF16), heads_ref[...]).astype(BF16)
        place = jnp.sum(hit * place_in, axis=1, keepdims=True) - 1.0
        ranks = jnp.where(place == well_lane, rank + 1.0, 0.0)
        for q in range(group):
            send_idx[i * group + q] = (
                jnp.sum(ranks[q * CAP : (q + 1) * CAP], axis=0, keepdims=True) - 1.0
            )

    pl.semaphore_wait(barrier, n_obs + n_cell - 2)

    def to_obs(src_of, dst, at):
        @pl.loop(1, n_obs)
        def _(i):
            to = lax.rem(o + i, n_obs)
            pltpu.make_async_remote_copy(
                src_ref=src_of(to), dst_ref=dst.at[o], send_sem=send_sem.at[at],
                recv_sem=recv_sem.at[at], device_id=(to, c), device_id_type=MESH,
            ).start()

        pltpu.make_async_copy(src_of(o), dst.at[o], recv_sem.at[at]).start()

    def to_cells(src_of, dst, at):
        @pl.loop(1, n_cell)
        def _(i):
            to = lax.rem(c + i, n_cell)
            pltpu.make_async_remote_copy(
                src_ref=src_of(to), dst_ref=dst.at[c], send_sem=send_sem.at[at],
                recv_sem=recv_sem.at[at], device_id=(o, to), device_id_type=MESH,
            ).start()

        pltpu.make_async_copy(src_of(c), dst.at[c], recv_sem.at[at]).start()

    line = n_cell * CAP
    to_obs(lambda to: send_heads.at[pl.ds(pl.multiple_of(to * line, line), line)], mid_heads, 0)
    to_obs(lambda to: send_idx.at[pl.ds(to * n_cell, n_cell)], mid_idx, 1)

    square = (members, members)
    centring = jnp.where(
        lax.broadcasted_iota(jnp.int32, square, 0) == lax.broadcasted_iota(jnp.int32, square, 1),
        1.0 - 1.0 / members, -1.0 / members,
    ).astype(BF16)
    step_rows = rows_per_step(piece_rows, 4096)
    squares[...] = jnp.zeros_like(squares)

    def covariance(p):
        piece_copy(p).wait()

        @pl.loop(0, piece_rows // step_rows)
        def _(i):
            at = pl.multiple_of(p * piece_rows + i * step_rows, step_rows)
            x = field[pl.ds(at, step_rows), :]
            anomalies = lax.dot_general(
                centring, x, (((1,), (1,)), ((), ())), preferred_element_type=F32
            )
            squares[...] += dot(anomalies.astype(BF16), x)

    def arrived(ref, at):
        pltpu.make_async_copy(ref, ref, recv_sem.at[at]).wait()

    eye = (
        lax.broadcasted_iota(jnp.int32, (wells, wells), 0)
        == lax.broadcasted_iota(jnp.int32, (wells, wells), 1)
    )
    inverse = 1.0 / jnp.sum(jnp.where(eye, std_ref[...], 0.0), axis=1, keepdims=True)
    tile_weights = [
        jnp.sum(
            jnp.where(loc_ref[...] == b * n_cell + c, taper_ref[...], 0.0),
            axis=1, keepdims=True,
        )
        for b in range(n_obs)
    ]

    covariance(0)
    arrived(mid_heads, 0)
    arrived(mid_idx, 1)
    to_cells(lambda to: mid_heads.at[:, pl.ds(pl.multiple_of(to * CAP, CAP), CAP)], recv_heads, 2)
    to_cells(lambda to: mid_idx.at[:, to], recv_idx, 6)
    covariance(1)
    arrived(recv_heads, 2)
    arrived(recv_idx, 6)
    ranks_at = lax.broadcasted_iota(jnp.int32, (total, CAP, wells), 1).astype(F32)
    ranks = recv_idx[...].reshape(total, 1, wells)
    take = jnp.where(ranks == ranks_at, 1.0, 0.0).reshape(total * CAP, wells)
    heads = recv_heads[...].reshape(total * CAP, members)
    pred = dot_rows(take.astype(BF16), heads)
    scaled = (pred - jnp.mean(pred, axis=1, keepdims=True)) * inverse
    innovation = (obs_ref[...] - pred) * inverse
    joined = jnp.concatenate([scaled, innovation], axis=1)
    part[...] = dot_rows(scaled, joined, HIGHEST).reshape(part.shape)
    to_obs(lambda to: part.at[to], bands, 4)
    covariance(2)
    arrived(bands, 4)
    for t in range(n_cell):
        terms[t] = sum(tile_weights[b][t : t + 1, :] * bands[b] for b in range(n_obs))
    to_cells(lambda to: terms.at[to], got, 3)
    covariance(3)
    covariance(4)
    arrived(got, 3)
    band_sum[...] = jnp.sum(got[...], axis=0)
    to_obs(lambda to: band_sum, summed, 5)
    covariance(5)
    arrived(summed, 5)
    gram_ref[...] = summed[...].reshape(gram_ref.shape)
    cov_ref[...] = squares[...] - jnp.mean(squares[...], axis=1, keepdims=True)

    def sent(ref, at):
        pltpu.make_async_copy(ref, ref, send_sem.at[at]).wait()

    sent(mid_heads.at[pl.ds(0, n_obs - 1)], 0)
    sent(mid_idx.at[pl.ds(0, n_obs - 1)], 1)
    sent(recv_heads.at[pl.ds(0, n_cell - 1)], 2)
    sent(recv_idx.at[pl.ds(0, n_cell - 1)], 6)
    sent(got.at[pl.ds(0, n_cell - 1)], 3)
    sent(bands.at[pl.ds(0, n_obs - 1)], 4)
    sent(summed.at[pl.ds(0, n_obs - 1)], 5)


def update_kernel(
    gram_ref, cov_ref, lambda_ref, log_k_ref, posterior_ref, norms_ref,
    field, inverse, weights, in_sem, out_sem,
):
    cells, members = field.shape
    groups = in_sem.shape[0]
    group_rows = cells // groups
    lambda_total = lambda_ref.shape[0]

    def group_copy(g, back):
        rows = pl.ds(g * group_rows, group_rows)
        if back:
            return pltpu.make_async_copy(field.at[rows], posterior_ref.at[rows], out_sem.at[g])
        return pltpu.make_async_copy(log_k_ref.at[rows], field.at[rows], in_sem.at[g])

    for g in range(groups):
        group_copy(g, False).start()

    curvature = gram_ref[:, :members]
    square = product(curvature, curvature)
    top = jnp.sqrt(jnp.max(jnp.sum(jnp.abs(square), axis=1, keepdims=True)))
    top = jnp.minimum(top, jnp.max(jnp.sum(jnp.abs(curvature), axis=1, keepdims=True)))
    cube = product(square, curvature)
    eye = jnp.where(
        lax.broadcasted_iota(jnp.int32, (members, members), 0)
        == lax.broadcasted_iota(jnp.int32, (members, members), 1),
        1.0, 0.0,
    )
    shifts = [(1.0 + lambda_ref[l]) * (members - 1) for l in range(lambda_total)]

    def advance(rho):
        return 2.0 / (2.0 - rho * rho), rho * rho / (2.0 - rho * rho)

    def block(l):
        return pl.ds(l * members, members)

    rhos = []
    for l in range(lambda_total):
        shift = shifts[l]
        first = 2.0 / (2.0 * shift + top)
        gain, rho = advance(top * (0.5 * first))
        u, v = 2.0 * gain * first, gain * first * first
        gain, rho = advance(rho)
        terms = (
            2.0 * u - 2.0 * v * shift - shift * (u - v * shift) * (u - v * shift),
            -2.0 * v - (u - v * shift) * (u - 3.0 * v * shift),
            v * (2.0 * u - 3.0 * v * shift),
            -v * v,
        )
        inverse[block(l), :] = gain * (
            terms[0] * eye + terms[1] * curvature + terms[2] * square + terms[3] * cube
        )
        rhos.append(rho)

    def largest(values):
        return functools.reduce(jnp.maximum, values)

    def step(carry):
        count, rhos = carry
        after = []
        shared = product(inverse[...], gram_ref[:, :members])
        for l in range(lambda_total):
            gain, rho = advance(rhos[l])
            x = inverse[block(l), :]
            half = shared[l * members : (l + 1) * members] + shifts[l] * x
            inverse[block(l), :] = gain * (2.0 * x - product(half, x))
            after.append(rho)
        return count + 1, tuple(after)

    lax.while_loop(
        lambda carry: (largest(carry[1]) > 3e-5) & (carry[0] < 40),
        step,
        (jnp.int32(0), tuple(rhos)),
    )

    solved = product(inverse[...], gram_ref[:, members:]).astype(BF16)
    transform = solved[:members].astype(F32)
    centred = transform - jnp.mean(transform, axis=0, keepdims=True) + eye
    high = centred.astype(BF16)
    low = (centred - high.astype(F32)).astype(BF16)
    none = jnp.zeros_like(high)
    weights[:members, :] = jnp.concatenate([high, none, low, none], axis=1)
    weights[members:, :] = jnp.concatenate([none, high, none, low], axis=1)

    step_rows = rows_per_step(group_rows, 4096)
    half_rows = step_rows // 2
    for g in range(groups):
        group_copy(g, False).wait()

        @pl.loop(0, group_rows // step_rows)
        def _(i):
            at = pl.multiple_of(g * group_rows + i * step_rows, step_rows)
            upper, lower = pl.ds(at, half_rows), pl.ds(at + half_rows, half_rows)
            x = jnp.concatenate([field[upper, :], field[lower, :]], axis=1)
            both = dot(x, weights[...])
            both = (both[:, : 2 * members] + both[:, 2 * members :]).astype(BF16)
            field[upper, :] = both[:, :members]
            field[lower, :] = both[:, members:]

        group_copy(g, True).start()

    beside = jnp.concatenate(
        [solved[l * members : (l + 1) * members] for l in range(lambda_total)], axis=1
    )
    high, middle, low = split(cov_ref[...])
    spread = dot(
        jnp.concatenate([high, middle], axis=1), jnp.concatenate([beside, beside], axis=0)
    ) + dot(low, beside)
    norms = jnp.sum(beside.astype(F32) * spread, axis=0, keepdims=True)
    for l in range(lambda_total):
        norms_ref[pl.ds(l, 1), :] = norms[:, l * members : (l + 1) * members]
    for g in range(groups):
        group_copy(g, True).wait()


def on_device(
    log_k, heads_pred, slot_well, tile_count, obs_values, obs_std, loc_blocks, taper, lambdas
):
    n_obs = lax.axis_size("obs")
    n_cell = lax.axis_size("cell")
    total = n_obs * n_cell
    cells, members = log_k.shape
    slots = slot_well.shape[0]
    wells = obs_values.shape[0]
    band = members // n_obs
    vmem = pl.BlockSpec(memory_space=pltpu.VMEM)
    smem = pl.BlockSpec(memory_space=pltpu.SMEM)
    hbm = pl.BlockSpec(memory_space=pl.ANY)
    gram, cov = pl.pallas_call(
        functools.partial(gram_kernel, n_obs, n_cell),
        out_shape=(
            jax.ShapeDtypeStruct((members, 2 * members), F32),
            jax.ShapeDtypeStruct((members, members), F32),
        ),
        in_specs=[hbm] * 8,
        out_specs=(vmem, vmem),
        scratch_shapes=[
            pltpu.VMEM((slots, members), BF16),
            pltpu.VMEM((1, slots), jnp.int32),
            pltpu.SMEM((1,), jnp.int32),
            pltpu.VMEM((1, wells), F32),
            pltpu.VMEM(loc_blocks.shape, jnp.int32),
            pltpu.VMEM(taper.shape, F32),
            pltpu.SemaphoreType.DMA((7,)),
            pltpu.VMEM((cells, members), BF16),
            pltpu.VMEM((members, members), F32),
            pltpu.VMEM((total * CAP, members), BF16),
            pltpu.VMEM((n_obs, n_cell * CAP, members), BF16),
            pltpu.VMEM((n_cell, n_obs, CAP, members), BF16),
            pltpu.VMEM((total, 1, wells), F32),
            pltpu.VMEM((n_obs, n_cell, 1, wells), F32),
            pltpu.VMEM((n_cell, n_obs, 1, wells), F32),
            pltpu.VMEM((wells, members), F32),
            pltpu.VMEM((n_obs, band, 2 * members), F32),
            pltpu.VMEM((n_cell, band, 2 * members), F32),
            pltpu.VMEM((n_cell, band, 2 * members), F32),
            pltpu.VMEM((n_obs, band, 2 * members), F32),
            pltpu.VMEM((band, 2 * members), F32),
            pltpu.VMEM((n_obs, band, 2 * members), F32),
            pltpu.SemaphoreType.DMA((PIECES,)),
            pltpu.SemaphoreType.DMA((7,)),
            pltpu.SemaphoreType.DMA((7,)),
        ],
        compiler_params=pltpu.CompilerParams(
            collective_id=0, has_side_effects=True, vmem_limit_bytes=60 << 20
        ),
        name="gram",
    )(
        heads_pred, slot_well.reshape(1, slots), tile_count, obs_values,
        obs_std.reshape(1, wells), loc_blocks, taper, log_k,
    )
    lambda_total = lambdas.shape[0]
    groups = 12
    posterior, norms = pl.pallas_call(
        update_kernel,
        out_shape=(
            jax.ShapeDtypeStruct((cells, members), BF16),
            jax.ShapeDtypeStruct((lambda_total, members), F32),
        ),
        in_specs=[vmem, vmem, smem, hbm],
        out_specs=(hbm, vmem),
        scratch_shapes=[
            pltpu.VMEM((cells, members), BF16),
            pltpu.VMEM((lambda_total * members, members), F32),
            pltpu.VMEM((2 * members, 4 * members), BF16),
            pltpu.SemaphoreType.DMA((groups,)),
            pltpu.SemaphoreType.DMA((groups,)),
        ],
        compiler_params=pltpu.CompilerParams(vmem_limit_bytes=60 << 20),
        name="update",
    )(gram, cov, lambdas, log_k)
    return posterior, norms[None]


def solution(mesh):
    return jax.shard_map(
        on_device,
        mesh=mesh,
        in_specs=(
            P(("obs", "cell"), None),
            P(("obs", "cell"), None),
            P(("obs", "cell")),
            P(("obs", "cell")),
            P(("obs", "cell"), None),
            P(("obs", "cell")),
            P(),
            P(),
            P(),
        ),
        out_specs=(P(("obs", "cell"), None), P(("obs", "cell"), None, None)),
        check_vma=False,
    )
```

```python
import functools

import jax
import jax.numpy as jnp
from jax import lax
from jax.experimental import pallas as pl
from jax.experimental.pallas import tpu as pltpu
from jax.sharding import PartitionSpec as P

CAP = 16
PIECES = 6
MESH = pl.DeviceIdType.MESH
HIGHEST = lax.Precision.HIGHEST
F32 = jnp.float32
BF16 = jnp.bfloat16


def dot(a, b, precision=None):
    return jnp.dot(a, b, precision=precision, preferred_element_type=F32)


def dot_rows(a, b, precision=None):
    return lax.dot_general(
        a, b, (((0,), (0,)), ((), ())), precision=precision, preferred_element_type=F32
    )


def split(x):
    high = x.astype(BF16)
    rest = x - high.astype(F32)
    middle = rest.astype(BF16)
    return high, middle, (rest - middle.astype(F32)).astype(BF16)


def product(a, b):
    a_high, a_middle, a_low = split(a)
    b_high, b_middle, b_low = split(b)
    pair = jnp.concatenate([b_high, b_middle], axis=1)
    large = dot(
        jnp.concatenate([a_high, a_middle], axis=1), jnp.concatenate([pair, pair], axis=0)
    )
    small = dot(
        jnp.concatenate([a_low, a_high], axis=1), jnp.concatenate([b_high, b_low], axis=0)
    )
    columns = b.shape[1]
    return large[:, :columns] + (large[:, columns:] + small)


def divide(x, n):
    if n & (n - 1) == 0:
        return lax.shift_right_logical(x, jnp.full(x.shape, n.bit_length() - 1, x.dtype))
    return x // n


def rows_per_step(total, most):
    step = most
    while total % step:
        step //= 2
    return step


def gram_kernel(
    n_obs, n_cell,
    heads_in, well_in, count_in, obs_in, std_in, loc_in, taper_in, log_k_ref,
    gram_ref, cov_ref,
    heads_ref, well_ref, count_ref, std_ref, loc_ref, taper_ref, in_sem, field, squares,
    send_heads, mid_heads, recv_heads, send_idx, mid_idx, recv_idx,
    obs_ref, part, terms, got, bands, band_sum, summed, field_sem, send_sem, recv_sem,
):
    total = n_obs * n_cell
    o, c = lax.axis_index("obs"), lax.axis_index("cell")
    cells, members = field.shape
    wells = obs_in.shape[0]
    slots = heads_ref.shape[0]
    piece_rows = cells // PIECES

    def piece_copy(p):
        rows = pl.ds(p * piece_rows, piece_rows)
        return pltpu.make_async_copy(log_k_ref.at[rows], field.at[rows], field_sem.at[p])

    inputs = [
        pltpu.make_async_copy(src, dst, in_sem.at[i])
        for i, (src, dst) in enumerate((
            (well_in, well_ref), (count_in, count_ref), (heads_in, heads_ref),
            (std_in, std_ref), (loc_in, loc_ref), (taper_in, taper_ref),
            (obs_in, obs_ref),
        ))
    ]
    for copy in inputs:
        copy.start()
    for p in range(PIECES):
        piece_copy(p).start()

    barrier = pltpu.get_barrier_semaphore()

    @pl.loop(1, n_obs)
    def _(i):
        pl.semaphore_signal(
            barrier, inc=1, device_id=(lax.rem(o + i, n_obs), c), device_id_type=MESH
        )

    @pl.loop(1, n_cell)
    def _(i):
        pl.semaphore_signal(
            barrier, inc=1, device_id=(o, lax.rem(c + i, n_cell)), device_id_type=MESH
        )

    for copy in inputs:
        copy.wait()

    well = well_ref[...]
    lane = lax.broadcasted_iota(jnp.int32, (1, slots), 1)
    owner = divide(well, wells)
    place_in = (well - owner * wells + 1).astype(F32)
    owner = jnp.where(lane < count_ref[0], owner, total)
    lane_f = lane.astype(F32)
    group = 8
    rows_now = group * CAP
    row_at = lax.broadcasted_iota(jnp.int32, (rows_now, 1), 0)
    in_group = divide(row_at, CAP)
    rank = (row_at - in_group * CAP).astype(F32)
    well_lane = lax.broadcasted_iota(jnp.int32, (1, wells), 1).astype(F32)

    @pl.loop(0, total // group)
    def _(i):
        dest = in_group + i * group
        start = jnp.sum(jnp.where(owner < dest, 1.0, 0.0), axis=1, keepdims=True)
        hit = jnp.where((owner == dest) & (lane_f == start + rank), 1.0, 0.0)
        rows = pl.ds(pl.multiple_of(i * rows_now, rows_now), rows_now)
        send_heads[rows, :] = dot(hit.astype(BF16), heads_ref[...]).astype(BF16)
        place = jnp.sum(hit * place_in, axis=1, keepdims=True) - 1.0
        ranks = jnp.where(place == well_lane, rank + 1.0, 0.0)
        for q in range(group):
            send_idx[i * group + q] = (
                jnp.sum(ranks[q * CAP : (q + 1) * CAP], axis=0, keepdims=True) - 1.0
            )

    pl.semaphore_wait(barrier, n_obs + n_cell - 2)

    def to_obs(src_of, dst, at):
        @pl.loop(1, n_obs)
        def _(i):
            to = lax.rem(o + i, n_obs)
            pltpu.make_async_remote_copy(
                src_ref=src_of(to), dst_ref=dst.at[o], send_sem=send_sem.at[at],
                recv_sem=recv_sem.at[at], device_id=(to, c), device_id_type=MESH,
            ).start()

        pltpu.make_async_copy(src_of(o), dst.at[o], recv_sem.at[at]).start()

    def to_cells(src_of, dst, at):
        @pl.loop(1, n_cell)
        def _(i):
            to = lax.rem(c + i, n_cell)
            pltpu.make_async_remote_copy(
                src_ref=src_of(to), dst_ref=dst.at[c], send_sem=send_sem.at[at],
                recv_sem=recv_sem.at[at], device_id=(o, to), device_id_type=MESH,
            ).start()

        pltpu.make_async_copy(src_of(c), dst.at[c], recv_sem.at[at]).start()

    line = n_cell * CAP
    to_obs(lambda to: send_heads.at[pl.ds(pl.multiple_of(to * line, line), line)], mid_heads, 0)
    to_obs(lambda to: send_idx.at[pl.ds(to * n_cell, n_cell)], mid_idx, 1)

    square = (members, members)
    centring = jnp.where(
        lax.broadcasted_iota(jnp.int32, square, 0) == lax.broadcasted_iota(jnp.int32, square, 1),
        1.0 - 1.0 / members, -1.0 / members,
    ).astype(BF16)
    step_rows = rows_per_step(piece_rows, 4096)
    squares[...] = jnp.zeros_like(squares)

    def covariance(p):
        piece_copy(p).wait()

        @pl.loop(0, piece_rows // step_rows)
        def _(i):
            at = pl.multiple_of(p * piece_rows + i * step_rows, step_rows)
            x = field[pl.ds(at, step_rows), :]
            anomalies = lax.dot_general(
                centring, x, (((1,), (1,)), ((), ())), preferred_element_type=F32
            )
            squares[...] += dot(anomalies.astype(BF16), x)

    def arrived(ref, at):
        pltpu.make_async_copy(ref, ref, recv_sem.at[at]).wait()

    eye = (
        lax.broadcasted_iota(jnp.int32, (wells, wells), 0)
        == lax.broadcasted_iota(jnp.int32, (wells, wells), 1)
    )
    inverse = 1.0 / jnp.sum(jnp.where(eye, std_ref[...], 0.0), axis=1, keepdims=True)
    tile_weights = [
        jnp.sum(
            jnp.where(loc_ref[...] == b * n_cell + c, taper_ref[...], 0.0),
            axis=1, keepdims=True,
        )
        for b in range(n_obs)
    ]

    covariance(0)
    arrived(mid_heads, 0)
    arrived(mid_idx, 1)
    to_cells(lambda to: mid_heads.at[:, pl.ds(pl.multiple_of(to * CAP, CAP), CAP)], recv_heads, 2)
    to_cells(lambda to: mid_idx.at[:, to], recv_idx, 6)
    covariance(1)
    arrived(recv_heads, 2)
    arrived(recv_idx, 6)
    ranks_at = lax.broadcasted_iota(jnp.int32, (total, CAP, wells), 1).astype(F32)
    ranks = recv_idx[...].reshape(total, 1, wells)
    take = jnp.where(ranks == ranks_at, 1.0, 0.0).reshape(total * CAP, wells)
    heads = recv_heads[...].reshape(total * CAP, members)
    pred = dot_rows(take.astype(BF16), heads)
    scaled = (pred - jnp.mean(pred, axis=1, keepdims=True)) * inverse
    innovation = (obs_ref[...] - pred) * inverse
    joined = jnp.concatenate([scaled, innovation], axis=1)
    part[...] = dot_rows(scaled, joined, HIGHEST).reshape(part.shape)
    to_obs(lambda to: part.at[to], bands, 4)
    covariance(2)
    arrived(bands, 4)
    for t in range(n_cell):
        terms[t] = sum(tile_weights[b][t : t + 1, :] * bands[b] for b in range(n_obs))
    to_cells(lambda to: terms.at[to], got, 3)
    covariance(3)
    covariance(4)
    arrived(got, 3)
    band_sum[...] = jnp.sum(got[...], axis=0)
    to_obs(lambda to: band_sum, summed, 5)
    covariance(5)
    arrived(summed, 5)
    gram_ref[...] = summed[...].reshape(gram_ref.shape)
    cov_ref[...] = squares[...] - jnp.mean(squares[...], axis=1, keepdims=True)

    def sent(ref, at):
        pltpu.make_async_copy(ref, ref, send_sem.at[at]).wait()

    sent(mid_heads.at[pl.ds(0, n_obs - 1)], 0)
    sent(mid_idx.at[pl.ds(0, n_obs - 1)], 1)
    sent(recv_heads.at[pl.ds(0, n_cell - 1)], 2)
    sent(recv_idx.at[pl.ds(0, n_cell - 1)], 6)
    sent(got.at[pl.ds(0, n_cell - 1)], 3)
    sent(bands.at[pl.ds(0, n_obs - 1)], 4)
    sent(summed.at[pl.ds(0, n_obs - 1)], 5)


def update_kernel(
    gram_ref, cov_ref, lambda_ref, log_k_ref, posterior_ref, norms_ref,
    field, inverse, weights, in_sem, out_sem,
):
    cells, members = field.shape
    groups = in_sem.shape[0]
    group_rows = cells // groups
    lambda_total = lambda_ref.shape[0]

    def group_copy(g, back):
        rows = pl.ds(g * group_rows, group_rows)
        if back:
            return pltpu.make_async_copy(field.at[rows], posterior_ref.at[rows], out_sem.at[g])
        return pltpu.make_async_copy(log_k_ref.at[rows], field.at[rows], in_sem.at[g])

    for g in range(groups):
        group_copy(g, False).start()

    curvature = gram_ref[:, :members]
    square = product(curvature, curvature)
    top = jnp.sqrt(jnp.max(jnp.sum(jnp.abs(square), axis=1, keepdims=True)))
    top = jnp.minimum(top, jnp.max(jnp.sum(jnp.abs(curvature), axis=1, keepdims=True)))
    cube = product(square, curvature)
    eye = jnp.where(
        lax.broadcasted_iota(jnp.int32, (members, members), 0)
        == lax.broadcasted_iota(jnp.int32, (members, members), 1),
        1.0, 0.0,
    )
    shifts = [(1.0 + lambda_ref[l]) * (members - 1) for l in range(lambda_total)]

    def advance(rho):
        return 2.0 / (2.0 - rho * rho), rho * rho / (2.0 - rho * rho)

    def block(l):
        return pl.ds(l * members, members)

    rhos = []
    for l in range(lambda_total):
        shift = shifts[l]
        first = 2.0 / (2.0 * shift + top)
        gain, rho = advance(top * (0.5 * first))
        u, v = 2.0 * gain * first, gain * first * first
        gain, rho = advance(rho)
        terms = (
            2.0 * u - 2.0 * v * shift - shift * (u - v * shift) * (u - v * shift),
            -2.0 * v - (u - v * shift) * (u - 3.0 * v * shift),
            v * (2.0 * u - 3.0 * v * shift),
            -v * v,
        )
        inverse[block(l), :] = gain * (
            terms[0] * eye + terms[1] * curvature + terms[2] * square + terms[3] * cube
        )
        rhos.append(rho)

    def largest(values):
        return functools.reduce(jnp.maximum, values)

    def step(carry):
        count, rhos = carry
        after = []
        shared = product(inverse[...], gram_ref[:, :members])
        for l in range(lambda_total):
            gain, rho = advance(rhos[l])
            x = inverse[block(l), :]
            half = shared[l * members : (l + 1) * members] + shifts[l] * x
            inverse[block(l), :] = gain * (2.0 * x - product(half, x))
            after.append(rho)
        return count + 1, tuple(after)

    lax.while_loop(
        lambda carry: (largest(carry[1]) > 3e-5) & (carry[0] < 40),
        step,
        (jnp.int32(0), tuple(rhos)),
    )

    solved = product(inverse[...], gram_ref[:, members:]).astype(BF16)
    transform = solved[:members].astype(F32)
    centred = transform - jnp.mean(transform, axis=0, keepdims=True) + eye
    high = centred.astype(BF16)
    low = (centred - high.astype(F32)).astype(BF16)
    none = jnp.zeros_like(high)
    weights[:members, :] = jnp.concatenate([high, none, low, none], axis=1)
    weights[members:, :] = jnp.concatenate([none, high, none, low], axis=1)

    step_rows = rows_per_step(group_rows, 2048)
    half_rows = step_rows // 2
    for g in range(groups):
        group_copy(g, False).wait()

        @pl.loop(0, group_rows // step_rows)
        def _(i):
            at = pl.multiple_of(g * group_rows + i * step_rows, step_rows)
            upper, lower = pl.ds(at, half_rows), pl.ds(at + half_rows, half_rows)
            x = jnp.concatenate([field[upper, :], field[lower, :]], axis=1)
            both = dot(x, weights[...])
            both = (both[:, : 2 * members] + both[:, 2 * members :]).astype(BF16)
            field[upper, :] = both[:, :members]
            field[lower, :] = both[:, members:]

        group_copy(g, True).start()

    beside = jnp.concatenate(
        [solved[l * members : (l + 1) * members] for l in range(lambda_total)], axis=1
    )
    high, middle, low = split(cov_ref[...])
    spread = dot(
        jnp.concatenate([high, middle], axis=1), jnp.concatenate([beside, beside], axis=0)
    ) + dot(low, beside)
    norms = jnp.sum(beside.astype(F32) * spread, axis=0, keepdims=True)
    for l in range(lambda_total):
        norms_ref[pl.ds(l, 1), :] = norms[:, l * members : (l + 1) * members]
    for g in range(groups):
        group_copy(g, True).wait()


def on_device(
    log_k, heads_pred, slot_well, tile_count, obs_values, obs_std, loc_blocks, taper, lambdas
):
    n_obs = lax.axis_size("obs")
    n_cell = lax.axis_size("cell")
    total = n_obs * n_cell
    cells, members = log_k.shape
    slots = slot_well.shape[0]
    wells = obs_values.shape[0]
    band = members // n_obs
    vmem = pl.BlockSpec(memory_space=pltpu.VMEM)
    smem = pl.BlockSpec(memory_space=pltpu.SMEM)
    hbm = pl.BlockSpec(memory_space=pl.ANY)
    gram, cov = pl.pallas_call(
        functools.partial(gram_kernel, n_obs, n_cell),
        out_shape=(
            jax.ShapeDtypeStruct((members, 2 * members), F32),
            jax.ShapeDtypeStruct((members, members), F32),
        ),
        in_specs=[hbm] * 8,
        out_specs=(vmem, vmem),
        scratch_shapes=[
            pltpu.VMEM((slots, members), BF16),
            pltpu.VMEM((1, slots), jnp.int32),
            pltpu.SMEM((1,), jnp.int32),
            pltpu.VMEM((1, wells), F32),
            pltpu.VMEM(loc_blocks.shape, jnp.int32),
            pltpu.VMEM(taper.shape, F32),
            pltpu.SemaphoreType.DMA((7,)),
            pltpu.VMEM((cells, members), BF16),
            pltpu.VMEM((members, members), F32),
            pltpu.VMEM((total * CAP, members), BF16),
            pltpu.VMEM((n_obs, n_cell * CAP, members), BF16),
            pltpu.VMEM((n_cell, n_obs, CAP, members), BF16),
            pltpu.VMEM((total, 1, wells), F32),
            pltpu.VMEM((n_obs, n_cell, 1, wells), F32),
            pltpu.VMEM((n_cell, n_obs, 1, wells), F32),
            pltpu.VMEM((wells, members), F32),
            pltpu.VMEM((n_obs, band, 2 * members), F32),
            pltpu.VMEM((n_cell, band, 2 * members), F32),
            pltpu.VMEM((n_cell, band, 2 * members), F32),
            pltpu.VMEM((n_obs, band, 2 * members), F32),
            pltpu.VMEM((band, 2 * members), F32),
            pltpu.VMEM((n_obs, band, 2 * members), F32),
            pltpu.SemaphoreType.DMA((PIECES,)),
            pltpu.SemaphoreType.DMA((7,)),
            pltpu.SemaphoreType.DMA((7,)),
        ],
        compiler_params=pltpu.CompilerParams(
            collective_id=0, has_side_effects=True, vmem_limit_bytes=60 << 20
        ),
        name="gram",
    )(
        heads_pred, slot_well.reshape(1, slots), tile_count, obs_values,
        obs_std.reshape(1, wells), loc_blocks, taper, log_k,
    )
    lambda_total = lambdas.shape[0]
    groups = 12
    posterior, norms = pl.pallas_call(
        update_kernel,
        out_shape=(
            jax.ShapeDtypeStruct((cells, members), BF16),
            jax.ShapeDtypeStruct((lambda_total, members), F32),
        ),
        in_specs=[vmem, vmem, smem, hbm],
        out_specs=(hbm, vmem),
        scratch_shapes=[
            pltpu.VMEM((cells, members), BF16),
            pltpu.VMEM((lambda_total * members, members), F32),
            pltpu.VMEM((2 * members, 4 * members), BF16),
            pltpu.SemaphoreType.DMA((groups,)),
            pltpu.SemaphoreType.DMA((groups,)),
        ],
        compiler_params=pltpu.CompilerParams(vmem_limit_bytes=60 << 20),
        name="update",
    )(gram, cov, lambdas, log_k)
    return posterior, norms[None]


def solution(mesh):
    return jax.shard_map(
        on_device,
        mesh=mesh,
        in_specs=(
            P(("obs", "cell"), None),
            P(("obs", "cell"), None),
            P(("obs", "cell")),
            P(("obs", "cell")),
            P(("obs", "cell"), None),
            P(("obs", "cell")),
            P(),
            P(),
            P(),
        ),
        out_specs=(P(("obs", "cell"), None), P(("obs", "cell"), None, None)),
        check_vma=False,
    )
```
